256 devices in a mesh: dp: 16 (over z_hi, y), tensor: 16 (over x, z_lo, core).
Axes of the slice: x: 4, y: 4, z: 8 (z_hi: 4, z_lo: 2; z = z_hi * 2 + z_lo), core: 2. Of those that a mesh axis runs over, the one named last changes fastest.
Arguments:
- x_rows: bfloat16 [12288, 4096], P(('dp', 'tensor')), may hold values from -24 to 24
- grad_out: bfloat16 [12288, 4096], P(('dp', 'tensor')), may hold values from -24 to 24
- gate_pre: bfloat16 [12288, 14336], P('dp', 'tensor'), may hold values from -8 to 8
- up_pre: bfloat16 [12288, 14336], P('dp', 'tensor'), may hold values from -6 to 6
- down_weight: bfloat16 [14336, 4096], P('tensor', 'dp'), may hold values from -0.046875 to 0.046875
Outputs:
- grad_gate: bfloat16 [12288, 14336], P('dp', 'tensor')
- grad_up: bfloat16 [12288, 14336], P('dp', 'tensor')
- grad_down: bfloat16 [14336, 4096], P('tensor', 'dp')
- gram_input: float32 [4096, 1024], P(('tensor', 'dp'))
- gram_output: float32 [4096, 1024], P(('tensor', 'dp'))
The draws below stay inside these ranges and needn't reach their ends.
All inputs are finite; a program needn't handle non-finite values.
Results may differ from the reference program's by a relative error of at most 0.0049.
Values may be sent and summed in bfloat16 or wider, within the bound.
A program may use at most 128 MiB of HBM per device.

```python
import jax
import jax.numpy as jnp
from jax import lax

D = 4096
FF = 14336
BLOCK = 1024
TOKENS = 12288


def spiked(result, stream_key, source, target, shards_of, factor):
    owner, partner = [(jnp.arange(result.shape[position]) // (result.shape[position] // shards_of)).reshape([-1 if axis == position else 1 for axis in range(result.ndim)]) for position in (source, target)]
    chosen = jax.random.permutation(stream_key, shards_of)[partner]
    strong = (owner == chosen) | (owner == (partner + shards_of // 2) % shards_of)
    return jnp.where(strong, factor * result, result)


def block_levels(rng, shape, pieces, low, top_value):
    def one(dim, blocks):
        heights = jax.random.uniform(jax.random.fold_in(jax.random.fold_in(rng, 6), dim), (blocks,), jnp.float32, low / len(pieces), top_value / len(pieces))
        return jnp.repeat(jnp.exp(heights), shape[dim] // blocks).reshape((-1,) + (1,) * (len(shape) - dim - 1))

    level = one(*pieces[0])
    for cut in pieces[1:]:
        level = level * one(*cut)
    return level


def normal_values(key, shape, spread, limit, cuts=(), kind=jnp.bfloat16):
    gain = block_levels(key, shape, cuts, -0.22, 0.18) if cuts else 1.0
    array = jax.random.normal(key, shape, jnp.float32) * spread * gain
    return jnp.minimum(jnp.maximum(array, -limit), limit).astype(kind)


def heavy_noise(key, extent, spread, reach, shards, heavy, kind=jnp.bfloat16):
    values = spread * jax.random.normal(key, extent, jnp.float32)
    if shards:
        values = values * block_levels(key, extent, shards, -0.22, 0.18)
    return jnp.clip(spiked(values, jax.random.fold_in(key, 3), *heavy), -reach, reach).astype(kind)


def setup_inputs(seed: int = 0) -> dict:
    key_of = jax.random.split(jax.random.key(seed), 6)
    return {
        "x_rows": heavy_noise(key_of[0], (TOKENS, D), 1.0, 24.0, ((0, 256),), (0, 1, 256, 6.0)),
        "grad_out": heavy_noise(key_of[1], (TOKENS, D), 1.0, 24.0, ((0, 256),), (0, 1, 256, 6.0)),
        "gate_pre": normal_values(key_of[2], (TOKENS, FF), 1.5, 8.0, ((0, 16), (1, 16))),
        "up_pre": normal_values(key_of[3], (TOKENS, FF), 1.0, 6.0, ((0, 16), (1, 16))),
        "down_weight": normal_values(key_of[4], (FF, D), FF ** -0.5, 0.046875, ((0, 16), (1, 16))),
    }


def block_gram(rows):

    def one_block(index):
        cols = lax.dynamic_slice_in_dim(rows, index * BLOCK, BLOCK, 1)
        return lax.dot_general(cols, cols, (((0,), (0,)), ((), ())), preferred_element_type=jnp.float32)
    blocks = lax.map(one_block, jnp.arange(D // BLOCK, dtype=jnp.int32))
    return blocks.reshape(D, BLOCK) / TOKENS

def reference(x_rows, grad_out, gate_pre, up_pre, down_weight):
    gate_f = gate_pre.astype(jnp.float32)
    up_f = up_pre.astype(jnp.float32)
    sigma = jax.nn.sigmoid(gate_f)
    silu = gate_f * sigma
    hidden = (silu * up_f).astype(jnp.bfloat16)
    grad_hidden = lax.dot_general(grad_out, down_weight, (((1,), (1,)), ((), ())), preferred_element_type=jnp.float32)
    grad_up = (grad_hidden * silu).astype(jnp.bfloat16)
    grad_gate = (grad_hidden * up_f * sigma * (1.0 + gate_f * (1.0 - sigma))).astype(jnp.bfloat16)
    scale = 1.0 / jnp.sqrt(jnp.float32(TOKENS))
    grad_down = (lax.dot_general(hidden, grad_out, (((0,), (0,)), ((), ())), preferred_element_type=jnp.float32) * scale).astype(jnp.bfloat16)
    return (grad_gate, grad_up, grad_down, block_gram(x_rows), block_gram(grad_out))
```

```python
import math

import jax
import jax.numpy as jnp
from jax import lax
from jax.experimental import pallas as pl
from jax.experimental.pallas import tpu as pltpu
from jax.sharding import PartitionSpec as P

MESH = pl.DeviceIdType.MESH
BF = jnp.bfloat16
F32 = jnp.float32
BLOCK = 1024


def kernel(
    total,
    x_ref, g_ref, gate_ref, up_ref, w_ref,
    gg_ref, gu_ref, gd_ref, gi_ref, go_ref,
    src, ghalf, tok, wf, ht, xb, asnd, arcv, part, zs, z1, z2,
    snd, rcv, ghf, gp, gbs, gbr, gas, gar, gf, gzs, gz1, gz2,
    ssem, rsem,
):
    rows = g_ref.shape[0]
    ffl, kc = w_ref.shape
    n_tok = gate_ref.shape[0]
    hk = kc // 2
    hf = ffl // 2
    d = lax.axis_index("dp")
    t = lax.axis_index("tensor")
    zh, y = d // 4, d % 4
    x, zl, c = t // 4, (t // 2) % 2, t % 2
    half = ((y + 1) // 2) % 2
    s = y // 2

    sib = (d, t + 1 - 2 * c)
    zlp = (d, t + 2 - 4 * zl)
    xr = (d, ((x + 1) % 4) * 4 + t % 4)
    xl = (d, ((x + 3) % 4) * 4 + t % 4)
    xo = (d, ((x + 2) % 4) * 4 + t % 4)
    ya = (zh * 4 + 3 - y, t)
    yb = (zh * 4 + y + 1 - 2 * (y % 2), t)
    zr = (((zh + 1) % 4) * 4 + y, t)
    zb = (((zh + 3) % 4) * 4 + y, t)
    neighbours = (sib, zlp, xr, xl, xo, ya, yb, zr, zb)

    barrier = pltpu.get_barrier_semaphore()
    for n in neighbours:
        pl.semaphore_signal(barrier, inc=1, device_id=n, device_id_type=MESH)
    pl.semaphore_wait(barrier, len(neighbours))

    names = {}
    started = []

    def sem(key):
        return names.setdefault(key, len(names))

    def send(key, src_ref, dst_ref, dev):
        k = sem(key)
        cp = pltpu.make_async_remote_copy(
            src_ref=src_ref, dst_ref=dst_ref, send_sem=ssem.at[k], recv_sem=rsem.at[k],
            device_id=dev, device_id_type=MESH,
        )
        cp.start()
        started.append(cp)

    def recv(key, dst_ref, dev):
        k = sem(key)
        pltpu.make_async_remote_copy(
            src_ref=dst_ref, dst_ref=dst_ref, send_sem=ssem.at[k], recv_sem=rsem.at[k],
            device_id=dev, device_id_type=MESH,
        ).wait_recv()

    def zz(r):
        return (zh + r) % 4

    def yy_of(h, q):
        return h + q * (3 - 2 * h)

    def wpiece(r, q, p):
        return wf.at[zz(r) * 2 + q, pl.ds(p * hk, hk), :]

    def w_to_a(r, p):
        send(("wa", r, p), wpiece(r, s, p), wpiece(r, s, p), ya)

    wf[zh * 2 + s] = w_ref[...].astype(F32).T.astype(BF)
    w_to_a(0, 0)
    send(("wl", 0), wpiece(0, s, 0), wpiece(0, s, 0), zr)
    send(("wr", 1), wpiece(0, s, 1), wpiece(0, s, 1), zb)
    w_to_a(0, 1)
    send(("wl", 1), wpiece(0, s, 1), wpiece(0, s, 1), zr)
    send(("wr", 0), wpiece(0, s, 0), wpiece(0, s, 0), zb)

    for z in range(4):
        for q in range(2):
            to = pl.ds((z * 2 + q) * kc, kc)
            other = pl.multiple_of((z * 4 + yy_of(1 - half, q)) * kc, kc)
            mine = pl.multiple_of((z * 4 + yy_of(half, q)) * kc, kc)
            ghalf[:, to] = g_ref[:, pl.ds(other, kc)]
            tok[0, x, zl, c, :, to] = g_ref[:, pl.ds(mine, kc)]

    def tpiece(slot, e, xx, cc=c):
        return tok.at[slot, xx, zl if e == 0 else 1 - zl, cc]

    x_left, x_right, x_opp = (x + 3) % 4, (x + 1) % 4, (x + 2) % 4

    def t_to_x(slot, e):
        ref = tpiece(slot, e, x)
        send(("txl", slot, e), ref, ref, xr)
        send(("txr", slot, e), ref, ref, xl)
        send(("ts", slot, e, 0), ref, ref, sib)

    send("tb", ghalf, tok.at[1, x, zl, c], yb)
    t_to_x(0, 0)
    send(("tz", 0), tpiece(0, 0, x), tpiece(0, 0, x), zlp)

    src[0] = x_ref[...]
    src[1] = g_ref[...]

    def block_cols(xx):
        return pl.ds(pl.multiple_of(xx * BLOCK, BLOCK), BLOCK)

    for r, dev in ((1, xr), (3, xl), (2, xo)):
        send(("gx", r), src.at[:, :, block_cols((x + r) % 4)], xb.at[c, zl, :, x], dev)
    xb[c, zl, :, x] = src[:, :, block_cols(x)]

    ht_tile = 128

    def hidden_tile(i):
        at = pl.ds(pl.multiple_of(i * ht_tile, ht_tile), ht_tile)
        gate = gate_ref[at, :].astype(F32)
        up = up_ref[at, :].astype(F32)
        hid = (gate * jax.nn.sigmoid(gate) * up).astype(BF)
        ht[0, :, at] = hid.astype(F32).T.astype(BF)

    n_ht = n_tok // ht_tile
    for p in range(2):
        pl.loop(p * n_ht // 2, (p + 1) * n_ht // 2)(hidden_tile)
        cols = pl.ds(p * n_tok // 2, n_tok // 2)
        send(("h", p), ht.at[0, :, cols], ht.at[1, :, cols], yb)

    recv("tb", tpiece(1, 0, x), yb)
    t_to_x(1, 0)
    send(("tz", 1), tpiece(1, 0, x), tpiece(1, 0, x), zlp)

    for r, dev in ((3, xr), (1, xl), (2, xo)):
        recv(("gx", r), xb.at[c, zl, :, (x + 4 - r) % 4], dev)
    send("gz", xb.at[c, zl], xb.at[c, zl], zlp)

    recv(("tz", 0), tpiece(0, 1, x), zlp)
    t_to_x(0, 1)

    def w_left(p):
        recv(("wl", p), wpiece(3, s, p), zb)
        if p == 0:
            send(("wo", 0), wpiece(3, s, 0), wpiece(3, s, 0), zr)
        w_to_a(3, p)

    def w_right(p):
        recv(("wr", p), wpiece(1, s, p), zr)
        if p == 1:
            send(("wo", 1), wpiece(1, s, 1), wpiece(1, s, 1), zb)
        w_to_a(1, p)

    def t_from_x(slot, e):
        left, right = tpiece(slot, e, x_left), tpiece(slot, e, x_right)
        recv(("txl", slot, e), left, xl)
        if slot == 0:
            send(("txo", slot, e), left, left, xr)
        send(("ts", slot, e, 3), left, left, sib)
        recv(("txr", slot, e), right, xr)
        if slot == 1:
            send(("txo", slot, e), right, right, xl)
        send(("ts", slot, e, 1), right, right, sib)

    def t_from_opp(slot, e):
        opp = tpiece(slot, e, x_opp)
        recv(("txo", slot, e), opp, xl if slot == 0 else xr)
        send(("ts", slot, e, 2), opp, opp, sib)

    t_from_x(0, 0)
    w_left(0)
    w_right(1)
    recv(("tz", 1), tpiece(1, 1, x), zlp)
    t_to_x(1, 1)
    t_from_x(1, 0)
    recv("gz", xb.at[c, 1 - zl], zlp)
    send("gs", xb.at[c], xb.at[c], sib)
    t_from_x(0, 1)
    w_left(1)
    w_right(0)
    t_from_opp(0, 0)
    t_from_opp(1, 0)

    recv("gs", xb.at[1 - c], sib)
    my_cols = pl.ds(pl.multiple_of((zl * 2 + c) * kc, kc), kc)
    for a in range(2):
        lhs = xb[:, :, a, :, :, my_cols].reshape(n_tok, kc)
        rhs = xb[:, :, a].reshape(n_tok, BLOCK)
        gram = lax.dot_general(lhs, rhs, (((0,), (0,)), ((), ())), preferred_element_type=F32)
        for z in range(4):
            for q in range(4):
                gp[q, z, a] = gram[(z * 4 + q) * 16:(z * 4 + q + 1) * 16, :]
    for q in range(2):
        gbs[q] = gp[yy_of(1 - half, q)].astype(BF)

    t_from_x(1, 1)
    for p in range(2):
        recv(("wo", p), wpiece(2, s, p), zb if p == 0 else zr)
        w_to_a(2, p)
    t_from_opp(0, 1)
    t_from_opp(1, 1)

    for slot in range(2):
        for e in range(2):
            for r in range(4):
                recv(("ts", slot, e, r), tpiece(slot, e, (x + r) % 4, 1 - c), sib)
    for p in range(2):
        cols = pl.ds(p * n_tok // 2, n_tok // 2)
        recv(("h", p), ht.at[1, :, cols], yb)
    send("gb", gbs, gbr, yb)

    scale = 1.0 / math.sqrt(total)

    def down(r, q):
        cols = pl.ds(pl.multiple_of((zz(r) * 2 + q) * kc, kc), kc)
        acc = jnp.dot(ht[0], tok[0, :, :, :, :, cols].reshape(n_tok, kc), preferred_element_type=F32)
        acc += jnp.dot(ht[1], tok[1, :, :, :, :, cols].reshape(n_tok, kc), preferred_element_type=F32)
        return acc * scale

    def dpiece(ref, i, p):
        return ref.at[i, pl.ds(p * hf, hf), :]

    def down_to_a(r):
        asnd[r] = down(r, 1 - s).astype(BF)
        for p in (1, 0) if r == 1 else (0, 1):
            send(("da", r, p), dpiece(asnd, r, p), dpiece(arcv, r, p), ya)

    n_tile = n_tok // 4

    def hidden_grad(slot, i):
        lhs = tok[slot, i].reshape(n_tile, kc * 8)
        return jnp.dot(lhs, wf[...].reshape(kc * 8, ffl), preferred_element_type=F32)

    def hidden_to_b(i):
        at = pl.ds(i * n_tile, n_tile)
        snd[at, :] = hidden_grad(1, i).astype(BF)
        send(("gh", i), snd.at[at, :], rcv.at[at, :], yb)

    down_to_a(2)
    part[2] = down(2, s)
    for r in range(4):
        for p in range(2):
            recv(("wa", r, p), wpiece(r, 1 - s, p), ya)
    hidden_to_b(0)
    down_to_a(1)
    hidden_to_b(1)
    down_to_a(3)
    hidden_to_b(2)
    down_to_a(0)

    def reduced(r, p):
        recv(("da", r, p), dpiece(arcv, r, p), ya)
        at = pl.ds(p * hf, hf)
        return part[r, at, :] + arcv[r, at, :].astype(F32)

    zs[0] = reduced(2, 0).astype(BF)
    send(("z1", 0), zs.at[0], z1.at[0], zr)
    zs[1] = reduced(2, 1).astype(BF)
    send(("z1", 1), zs.at[1], z1.at[1], zb)
    hidden_to_b(3)
    part[1] = down(1, s)
    part[3] = down(3, s)

    recv("gb", gbr, yb)
    gas[...] = (gp[yy_of(half, 1 - s)] + gbr[1 - s].astype(F32)).astype(BF)
    send("ga", gas, gar, ya)
    gf[...] = gp[yy_of(half, s)] + gbr[s].astype(F32)

    zs[2] = reduced(1, 1).astype(BF)
    send(("z2r", 1), zs.at[2], dpiece(z2, 0, 1), zr)
    part[0] = down(0, s)
    zs[3] = reduced(3, 0).astype(BF)
    send(("z2l", 0), zs.at[3], dpiece(z2, 1, 0), zb)
    recv(("z1", 0), z1.at[0], zb)
    zs[4] = (reduced(1, 0) + z1[0].astype(F32)).astype(BF)
    send(("z2r", 0), zs.at[4], dpiece(z2, 0, 0), zr)
    recv(("z1", 1), z1.at[1], zr)
    zs[5] = (reduced(3, 1) + z1[1].astype(F32)).astype(BF)
    send(("z2l", 1), zs.at[5], dpiece(z2, 1, 1), zb)

    recv("ga", gar, ya)
    gf[...] += gar[...].astype(F32)
    gzs[0, 0] = gf[zz(2), 0].astype(BF)
    gzs[0, 1] = gf[zz(2), 1].astype(BF)
    send(("gz1", 0), gzs.at[0, 0], gz1.at[0], zr)
    send(("gz1", 1), gzs.at[0, 1], gz1.at[1], zb)

    for i in range(4):
        at = pl.ds(i * n_tile, n_tile)
        ghf[at, :] = hidden_grad(0, i)

    recv(("gz1", 0), gz1.at[0], zb)
    gzs[1, 0] = (gf[zz(1), 0] + gz1[0].astype(F32)).astype(BF)
    gzs[1, 1] = gf[zz(1), 1].astype(BF)
    send("gz2r", gzs.at[1], gz2.at[0], zr)
    recv(("gz1", 1), gz1.at[1], zr)
    gzs[2, 0] = gf[zz(3), 0].astype(BF)
    gzs[2, 1] = (gf[zz(3), 1] + gz1[1].astype(F32)).astype(BF)
    send("gz2l", gzs.at[2], gz2.at[1], zb)

    step = 32
    for i in range(4):
        at = pl.ds(i * n_tile, n_tile)
        recv(("gh", i), rcv.at[at, :], yb)

        @pl.loop(0, n_tile // step)
        def _(k):
            rows_at = pl.ds(pl.multiple_of(i * n_tile + k * step, step), step)
            gh = ghf[rows_at, :] + rcv[rows_at, :].astype(F32)
            gate = gate_ref[rows_at, :].astype(F32)
            up = up_ref[rows_at, :].astype(F32)
            sigma = jax.nn.sigmoid(gate)
            gu_ref[rows_at, :] = (gh * (gate * sigma)).astype(BF)
            gg_ref[rows_at, :] = (gh * up * sigma * (1.0 + gate * (1.0 - sigma))).astype(BF)

    recv("gz2r", gz2.at[0], zb)
    recv("gz2l", gz2.at[1], zr)
    for a, out in ((0, gi_ref), (1, go_ref)):
        out[...] = (gf[zh, a] + gz2[0, a].astype(F32) + gz2[1, a].astype(F32)) / total

    for p in range(2):
        at = pl.ds(p * hf, hf)
        recv(("z2r", p), dpiece(z2, 0, p), zb)
        recv(("z2l", p), dpiece(z2, 1, p), zr)
        own = reduced(0, p) + z2[0, at, :].astype(F32) + z2[1, at, :].astype(F32)
        gd_ref[at, :] = own.astype(BF)

    for cp in started:
        cp.wait_send()
    assert len(names) <= N_SEM, len(names)


N_SEM = 96


def shards(x_rows, grad_out, gate_pre, up_pre, down_weight):
    rows, width = x_rows.shape
    n_tok, ffl = gate_pre.shape
    kc = down_weight.shape[1]
    hf = ffl // 2
    total = float(rows * lax.axis_size("tensor") * lax.axis_size("dp"))
    gr = kc // 16
    vmem = pl.BlockSpec(memory_space=pltpu.VMEM)

    def kern(*refs):
        kernel(total, *refs)

    return pl.pallas_call(
        kern,
        out_shape=(
            jax.ShapeDtypeStruct((n_tok, ffl), BF),
            jax.ShapeDtypeStruct((n_tok, ffl), BF),
            jax.ShapeDtypeStruct((ffl, kc), BF),
            jax.ShapeDtypeStruct((gr, BLOCK), F32),
            jax.ShapeDtypeStruct((gr, BLOCK), F32),
        ),
        in_specs=[vmem] * 5,
        out_specs=(vmem,) * 5,
        scratch_shapes=[
            pltpu.VMEM((2, rows, width), BF),
            pltpu.VMEM((rows, kc * 8), BF),
            pltpu.VMEM((2, 4, 2, 2, rows, kc * 8), BF),
            pltpu.VMEM((8, kc, ffl), BF),
            pltpu.VMEM((2, ffl, n_tok), BF),
            pltpu.VMEM((2, 2, 2, 4, rows, BLOCK), BF),
            pltpu.VMEM((4, ffl, kc), BF),
            pltpu.VMEM((4, ffl, kc), BF),
            pltpu.VMEM((4, ffl, kc), F32),
            pltpu.VMEM((6, hf, kc), BF),
            pltpu.VMEM((2, hf, kc), BF),
            pltpu.VMEM((2, ffl, kc), BF),
            pltpu.VMEM((n_tok, ffl), BF),
            pltpu.VMEM((n_tok, ffl), BF),
            pltpu.VMEM((n_tok, ffl), F32),
            pltpu.VMEM((4, 4, 2, gr, BLOCK), F32),
            pltpu.VMEM((2, 4, 2, gr, BLOCK), BF),
            pltpu.VMEM((2, 4, 2, gr, BLOCK), BF),
            pltpu.VMEM((4, 2, gr, BLOCK), BF),
            pltpu.VMEM((4, 2, gr, BLOCK), BF),
            pltpu.VMEM((4, 2, gr, BLOCK), F32),
            pltpu.VMEM((3, 2, gr, BLOCK), BF),
            pltpu.VMEM((2, gr, BLOCK), BF),
            pltpu.VMEM((2, 2, gr, BLOCK), BF),
            pltpu.SemaphoreType.DMA((N_SEM,)),
            pltpu.SemaphoreType.DMA((N_SEM,)),
        ],
        compiler_params=pltpu.CompilerParams(
            collective_id=0, has_side_effects=True, vmem_limit_bytes=60 * 1024 * 1024
        ),
        cost_estimate=pl.CostEstimate(
            flops=4 * n_tok * width * ffl, bytes_accessed=8 * n_tok * ffl, transcendentals=0
        ),
    )(x_rows, grad_out, gate_pre, up_pre, down_weight)


def solution(mesh):
    return jax.shard_map(
        shards,
        mesh=mesh,
        in_specs=(
            P(("dp", "tensor"), None),
            P(("dp", "tensor"), None),
            P("dp", "tensor"),
            P("dp", "tensor"),
            P("tensor", "dp"),
        ),
        out_specs=(
            P("dp", "tensor"),
            P("dp", "tensor"),
            P("tensor", "dp"),
            P(("tensor", "dp"), None),
            P(("tensor", "dp"), None),
        ),
        check_vma=False,
    )
```

```python
import math

import jax
import jax.numpy as jnp
from jax import lax
from jax.experimental import pallas as pl
from jax.experimental.pallas import tpu as pltpu
from jax.sharding import PartitionSpec as P

MESH = pl.DeviceIdType.MESH
BF = jnp.bfloat16
F32 = jnp.float32
BLOCK = 1024
N_SEM = 128
SPLIT = 512


def kernel(
    total,
    x_hbm, g_hbm, gate_hbm, up_hbm, w_hbm,
    gg_hbm, gu_hbm, gd_hbm, gi_hbm, go_hbm,
    x_ref, g_ref, gate_ref, up_ref, w_ref,
    gg_ref, gu_ref, gd_ref, gi_ref, go_ref,
    ghalf, tok, wf0, wf1, ht, xi, xo_buf, gm, asnd, arcv, part, zs, z1, z2,
    snd0, snd1, rcv0, rcv1, ghf, gp, gbs, gbr, gas, gar, gf, gzs, gz1, gz2,
    ssem, rsem, isem, osem,
):
    rows = g_ref.shape[0]
    ffl, kc = w_ref.shape
    n_tok = gate_ref.shape[0]
    hk = kc // 2
    hf = ffl // 2
    hcols = (pl.ds(0, SPLIT), pl.ds(SPLIT, ffl - SPLIT))
    d = lax.axis_index("dp")
    t = lax.axis_index("tensor")
    zh, y = d // 4, d % 4
    x, zl, c = t // 4, (t // 2) % 2, t % 2
    half = ((y + 1) // 2) % 2
    s = y // 2

    sib = (d, t + 1 - 2 * c)
    zlp = (d, t + 2 - 4 * zl)
    xr = (d, ((x + 1) % 4) * 4 + t % 4)
    xl = (d, ((x + 3) % 4) * 4 + t % 4)
    xo = (d, ((x + 2) % 4) * 4 + t % 4)
    ya = (zh * 4 + 3 - y, t)
    yb = (zh * 4 + y + 1 - 2 * (y % 2), t)
    zr = (((zh + 1) % 4) * 4 + y, t)
    zb = (((zh + 3) % 4) * 4 + y, t)
    zo = (((zh + 3 + 2 * zl) % 4) * 4 + y, t + 2 - 4 * zl)
    neighbours = (sib, zlp, zo, xr, xl, xo, ya, yb, zr, zb)

    barrier = pltpu.get_barrier_semaphore()
    for n in neighbours:
        pl.semaphore_signal(barrier, inc=1, device_id=n, device_id_type=MESH)
    loads = [
        pltpu.make_async_copy(a, b, isem.at[i])
        for i, (a, b) in enumerate(
            ((w_hbm, w_ref), (g_hbm, g_ref), (gate_hbm, gate_ref), (up_hbm, up_ref), (x_hbm, x_ref))
        )
    ]
    for cp in loads:
        cp.start()

    names = {}
    started = []
    stores = []

    def sem(key):
        return names.setdefault(key, len(names))

    def send(key, src_ref, dst_ref, dev):
        k = sem(key)
        cp = pltpu.make_async_remote_copy(
            src_ref=src_ref, dst_ref=dst_ref, send_sem=ssem.at[k], recv_sem=rsem.at[k],
            device_id=dev, device_id_type=MESH,
        )
        cp.start()
        started.append(cp)

    def recv(key, dst_ref, dev):
        k = sem(key)
        pltpu.make_async_remote_copy(
            src_ref=dst_ref, dst_ref=dst_ref, send_sem=ssem.at[k], recv_sem=rsem.at[k],
            device_id=dev, device_id_type=MESH,
        ).wait_recv()

    def store(src_ref, dst_ref):
        cp = pltpu.make_async_copy(src_ref, dst_ref, osem.at[len(stores)])
        cp.start()
        stores.append(cp)

    def zz(r):
        return (zh + r) % 4

    def yy_of(h, q):
        return h + q * (3 - 2 * h)

    def wpiece(r, q, hh, kh=None):
        ref = (wf0, wf1)[hh]
        if kh is None:
            return ref.at[zz(r) * 2 + q]
        return ref.at[zz(r) * 2 + q, pl.ds(kh * hk, hk), :]

    def w_to_a(r, hh, kh=None):
        send(("wa", r, hh, kh), wpiece(r, s, hh, kh), wpiece(r, s, hh, kh), ya)

    def w_own(hh, i):
        send(("wl", hh, i), wpiece(0, s, hh, i), wpiece(0, s, hh, i), zr)
        send(("wr", hh, i), wpiece(0, s, hh, 1 - i), wpiece(0, s, hh, 1 - i), zb)

    def w_mid(hh, i):
        recv(("wl", hh, i), wpiece(3, s, hh, i), zb)
        if i == 0:
            send(("wo", hh, 0), wpiece(3, s, hh, 0), wpiece(3, s, hh, 0), zr)
        recv(("wr", hh, i), wpiece(1, s, hh, 1 - i), zr)
        if i == 0:
            send(("wo", hh, 1), wpiece(1, s, hh, 1), wpiece(1, s, hh, 1), zb)
        w_to_a(3, hh, i)
        w_to_a(1, hh, 1 - i)

    def w_opp(hh, kh):
        recv(("wo", hh, kh), wpiece(2, s, hh, kh), zb if kh == 0 else zr)
        w_to_a(2, hh, kh)

    def w_from_a(hh):
        recv(("wa", 0, hh, None), wpiece(0, 1 - s, hh), ya)
        for r in (3, 1, 2):
            for kh in range(2):
                recv(("wa", r, hh, kh), wpiece(r, 1 - s, hh, kh), ya)

    loads[0].wait()
    wf0[zh * 2 + s] = w_ref[:SPLIT, :].astype(F32).T.astype(BF)
    wf1[zh * 2 + s] = w_ref[SPLIT:, :].astype(F32).T.astype(BF)

    loads[1].wait()
    for z in range(4):
        for q in range(2):
            to = pl.ds((z * 2 + q) * kc, kc)
            other = pl.multiple_of((z * 4 + yy_of(1 - half, q)) * kc, kc)
            mine = pl.multiple_of((z * 4 + yy_of(half, q)) * kc, kc)
            ghalf[:, to] = g_ref[:, pl.ds(other, kc)]
            tok[0, x, zl, c, :, to] = g_ref[:, pl.ds(mine, kc)]

    pl.semaphore_wait(barrier, len(neighbours))

    w_to_a(0, 0)
    w_own(0, 0)
    w_own(0, 1)

    def tpiece(slot, e, xx, cc=c):
        return tok.at[slot, xx, zl if e == 0 else 1 - zl, cc]

    x_left, x_right, x_opp = (x + 3) % 4, (x + 1) % 4, (x + 2) % 4

    def t_to_x(slot, e):
        ref = tpiece(slot, e, x)
        send(("txl", slot, e), ref, ref, xr)
        send(("txr", slot, e), ref, ref, xl)
        send(("ts", slot, e, 0), ref, ref, sib)

    def t_from_x(slot, e):
        left, right = tpiece(slot, e, x_left), tpiece(slot, e, x_right)
        recv(("txl", slot, e), left, xl)
        if slot == 0:
            send(("txo", slot, e), left, left, xr)
        send(("ts", slot, e, 3), left, left, sib)
        recv(("txr", slot, e), right, xr)
        if slot == 1:
            send(("txo", slot, e), right, right, xl)
        send(("ts", slot, e, 1), right, right, sib)

    def t_from_opp(slot, e):
        opp = tpiece(slot, e, x_opp)
        recv(("txo", slot, e), opp, xl if slot == 0 else xr)
        send(("ts", slot, e, 2), opp, opp, sib)

    def t_to_z(slot):
        send(("tz", slot), tpiece(slot, 0, x), tpiece(slot, 0, x), zlp)

    send("tb", ghalf, tok.at[1, x, zl, c], yb)
    t_to_x(0, 0)
    w_to_a(0, 1)

    loads[2].wait()
    loads[3].wait()
    ht_tile = 128

    def hidden_tile(i):
        at = pl.ds(pl.multiple_of(i * ht_tile, ht_tile), ht_tile)
        gate = gate_ref[at, :].astype(F32)
        up = up_ref[at, :].astype(F32)
        hid = (gate * jax.nn.sigmoid(gate) * up).astype(BF)
        ht[0, :, at] = hid.astype(F32).T.astype(BF)

    n_ht = n_tok // ht_tile
    for p in range(2):
        pl.loop(p * n_ht // 2, (p + 1) * n_ht // 2)(hidden_tile)
        cols = pl.ds(p * n_tok // 2, n_tok // 2)
        send(("h", p), ht.at[0, :, cols], ht.at[1, :, cols], yb)

    loads[4].wait()

    def x_cols(xx):
        return pl.ds(pl.multiple_of(xx * BLOCK, BLOCK), BLOCK)

    def o_cols(xx):
        return pl.ds(pl.multiple_of(xx * 2 * kc, 2 * kc), 2 * kc)

    xi[c, zl, x] = x_ref[:, x_cols(x)]
    xo_buf[c, zl, x] = ghalf[:, o_cols(x)]
    for r, dev in ((1, xr), (3, xl), (2, xo)):
        send(("gxi", r), x_ref.at[:, x_cols((x + r) % 4)], xi.at[c, zl, x], dev)

    recv("tb", tpiece(1, 0, x), yb)
    t_to_x(1, 0)
    w_mid(0, 0)
    t_from_x(0, 0)
    w_mid(0, 1)
    t_to_z(0)
    t_to_z(1)
    for r, dev in ((3, xr), (1, xl), (2, xo)):
        recv(("gxi", r), xi.at[c, zl, (x + 4 - r) % 4], dev)
    send("gzi", xi.at[c, zl], xi.at[c, zl], zo)
    t_from_x(1, 0)
    w_opp(0, 0)
    w_opp(0, 1)
    w_own(1, 0)
    recv(("tz", 0), tpiece(0, 1, x), zlp)
    t_to_x(0, 1)
    recv(("tz", 1), tpiece(1, 1, x), zlp)
    t_to_x(1, 1)
    w_own(1, 1)
    t_from_x(0, 1)
    recv("gzi", xi.at[c, 1 - zl], zo)
    send("gsi", xi.at[c], xi.at[c], sib)
    w_mid(1, 0)
    t_from_x(1, 1)
    for r, dev in ((1, xr), (3, xl), (2, xo)):
        send(("gxo", r), ghalf.at[:, o_cols((x + r) % 4)], xo_buf.at[c, zl, x], dev)

    recv("gsi", xi.at[1 - c], sib)
    my_cols = pl.ds(pl.multiple_of((zl * 2 + c) * kc, kc), kc)

    def gram(a, ref):
        lhs, rhs = ref[:, :, :, :, my_cols].reshape(n_tok, kc), ref[...].reshape(n_tok, BLOCK)
        out = lax.dot_general(lhs, rhs, (((0,), (0,)), ((), ())), preferred_element_type=F32)
        for z in range(4):
            for q in range(4):
                gp[a, q, z] = out[(z * 4 + q) * 16:(z * 4 + q + 1) * 16, :]
        for q in range(2):
            gbs[a, q] = gp[a, yy_of(1 - half, q)].astype(BF)

    gram(0, xi)
    w_mid(1, 1)
    t_from_opp(0, 0)
    t_from_opp(1, 0)
    t_from_opp(0, 1)
    t_from_opp(1, 1)
    w_opp(1, 0)
    w_opp(1, 1)
    for r, dev in ((3, xr), (1, xl), (2, xo)):
        recv(("gxo", r), xo_buf.at[c, zl, (x + 4 - r) % 4], dev)
    send("gzo", xo_buf.at[c, zl], xo_buf.at[c, zl], zlp)
    for p in range(2):
        cols = pl.ds(p * n_tok // 2, n_tok // 2)
        recv(("h", p), ht.at[1, :, cols], yb)
    send(("gb", 0), gbs.at[0], gbr.at[0], yb)

    for slot in range(2):
        for e in range(2):
            for r in range(4):
                recv(("ts", slot, e, r), tpiece(slot, e, (x + r) % 4, 1 - c), sib)

    scale = 1.0 / math.sqrt(total)

    def down(r, q):
        cols = pl.ds(pl.multiple_of((zz(r) * 2 + q) * kc, kc), kc)
        acc = jnp.dot(ht[0], tok[0, :, :, :, :, cols].reshape(n_tok, kc), preferred_element_type=F32)
        acc += jnp.dot(ht[1], tok[1, :, :, :, :, cols].reshape(n_tok, kc), preferred_element_type=F32)
        return acc * scale

    def dpiece(ref, i, p):
        return ref.at[i, pl.ds(p * hf, hf), :]

    def down_to_a(r, p):
        send(("da", r, p), dpiece(asnd, r, p), dpiece(arcv, r, p), ya)

    n_tile = n_tok // 2

    def hidden_grad(slot, hh, i):
        lhs = tok[slot, 2 * i:2 * i + 2].reshape(n_tile, kc * 8)
        rhs = wf0[...].reshape(kc * 8, SPLIT) if hh == 0 else wf1[...].reshape(kc * 8, ffl - SPLIT)
        return jnp.dot(lhs, rhs, preferred_element_type=F32)

    def hidden_to_b(hh, i):
        at = pl.ds(i * n_tile, n_tile)
        snd, rcv = (snd0, snd1)[hh], (rcv0, rcv1)[hh]
        send(("gh", hh, i), snd.at[at, :], rcv.at[at, :], yb)

    w_from_a(0)
    for i in range(2):
        snd0[i * n_tile:(i + 1) * n_tile, :] = hidden_grad(1, 0, i).astype(BF)
        hidden_to_b(0, i)
    asnd[2] = down(2, 1 - s).astype(BF)
    down_to_a(2, 0)
    down_to_a(2, 1)
    asnd[1] = down(1, 1 - s).astype(BF)
    asnd[3] = down(3, 1 - s).astype(BF)
    part[2] = down(2, s)
    w_from_a(1)
    for i in range(2):
        snd1[i * n_tile:(i + 1) * n_tile, :] = hidden_grad(1, 1, i).astype(BF)

    def reduced(r, p):
        recv(("da", r, p), dpiece(arcv, r, p), ya)
        at = pl.ds(p * hf, hf)
        return part[r, at, :] + arcv[r, at, :].astype(F32)

    def gram_to_a(a):
        recv(("gb", a), gbr.at[a], yb)
        gas[a] = (gp[a, yy_of(half, 1 - s)] + gbr[a, 1 - s].astype(F32)).astype(BF)
        send(("ga", a), gas.at[a], gar.at[a], ya)
        gf[a] = gp[a, yy_of(half, s)] + gbr[a, s].astype(F32)

    def gram_z1(a):
        recv(("ga", a), gar.at[a], ya)
        gf[a] = gf[a] + gar[a].astype(F32)
        gzs[a, 0] = gf[a, zz(2)].astype(BF)
        send(("gz1", a), gzs.at[a, 0], gz1.at[a], zr if a == 0 else zb)

    def gram_z2(a):
        recv(("gz1", a), gz1.at[a], zb if a == 0 else zr)
        passed = gz1[a].astype(F32)
        gzs[a, 1] = (gf[a, zz(1)] + passed if a == 0 else gf[a, zz(1)]).astype(BF)
        send(("gz2r", a), gzs.at[a, 1], gz2.at[a, 0], zr)
        gzs[a, 2] = (gf[a, zz(3)] + passed if a == 1 else gf[a, zz(3)]).astype(BF)
        send(("gz2l", a), gzs.at[a, 2], gz2.at[a, 1], zb)

    def gram_out(a, out, hbm):
        recv(("gz2r", a), gz2.at[a, 0], zb)
        recv(("gz2l", a), gz2.at[a, 1], zr)
        out[...] = (gf[a, zh] + gz2[a, 0].astype(F32) + gz2[a, 1].astype(F32)) / total
        store(out, hbm)

    gram_to_a(0)
    recv("gzo", xo_buf.at[c, 1 - zl], zlp)
    send("gso", xo_buf.at[c], xo_buf.at[c], sib)
    for q in range(2):
        mine = pl.ds(pl.multiple_of(yy_of(half, q) * kc, kc), kc)
        from_tok = pl.ds(pl.multiple_of((x * 2 + q) * kc, kc), kc)
        for cc in range(2):
            for zc in range(2):
                for xc in range(4):
                    gm[cc, zc, xc, :, mine] = tok[0, xc, zc, cc, :, from_tok]
    recv("gso", xo_buf.at[1 - c], sib)
    for q in range(2):
        other = pl.ds(pl.multiple_of(yy_of(1 - half, q) * kc, kc), kc)
        gm[:, :, :, :, other] = xo_buf[:, :, :, :, q * kc:(q + 1) * kc]
    gram(1, gm)
    send(("gb", 1), gbs.at[1], gbr.at[1], yb)
    hidden_to_b(1, 0)
    hidden_to_b(1, 1)

    zs[0] = reduced(2, 0).astype(BF)
    send(("z1", 0), zs.at[0], z1.at[0], zr)
    down_to_a(1, 1)
    down_to_a(3, 0)
    zs[1] = reduced(2, 1).astype(BF)
    send(("z1", 1), zs.at[1], z1.at[1], zb)
    down_to_a(1, 0)
    down_to_a(3, 1)
    gram_z1(0)
    part[1] = down(1, s)
    part[3] = down(3, s)
    asnd[0] = down(0, 1 - s).astype(BF)
    gram_z2(0)
    gram_to_a(1)
    zs[2] = reduced(1, 1).astype(BF)
    send(("z2r", 1), zs.at[2], dpiece(z2, 0, 1), zr)
    zs[3] = reduced(3, 0).astype(BF)
    send(("z2l", 0), zs.at[3], dpiece(z2, 1, 0), zb)
    down_to_a(0, 0)
    down_to_a(0, 1)
    gram_z1(1)

    recv(("z1", 0), z1.at[0], zb)
    zs[4] = (reduced(1, 0) + z1[0].astype(F32)).astype(BF)
    send(("z2r", 0), zs.at[4], dpiece(z2, 0, 0), zr)
    recv(("z1", 1), z1.at[1], zr)
    zs[5] = (reduced(3, 1) + z1[1].astype(F32)).astype(BF)
    send(("z2l", 1), zs.at[5], dpiece(z2, 1, 1), zb)

    part[0] = down(0, s)
    for hh in range(2):
        for i in range(2):
            ghf[i * n_tile:(i + 1) * n_tile, hcols[hh]] = hidden_grad(0, hh, i)

    step = 32

    def finish(hh):
        rcv, cols = (rcv0, rcv1)[hh], hcols[hh]
        for i in range(2):
            at = pl.ds(i * n_tile, n_tile)
            recv(("gh", hh, i), rcv.at[at, :], yb)

            @pl.loop(0, n_tile // step)
            def _(k):
                rows_at = pl.ds(pl.multiple_of(i * n_tile + k * step, step), step)
                gh = ghf[rows_at, cols] + rcv[rows_at, :].astype(F32)
                gate = gate_ref[rows_at, cols].astype(F32)
                up = up_ref[rows_at, cols].astype(F32)
                sigma = jax.nn.sigmoid(gate)
                gu_ref[rows_at, cols] = (gh * (gate * sigma)).astype(BF)
                gg_ref[rows_at, cols] = (gh * up * sigma * (1.0 + gate * (1.0 - sigma))).astype(BF)

            store(gu_ref.at[at, cols], gu_hbm.at[at, cols])
            store(gg_ref.at[at, cols], gg_hbm.at[at, cols])

    finish(0)

    gram_z2(1)
    gram_out(0, gi_ref, gi_hbm)
    finish(1)
    gram_out(1, go_ref, go_hbm)

    for p in range(2):
        at = pl.ds(p * hf, hf)
        recv(("z2r", p), dpiece(z2, 0, p), zb)
        recv(("z2l", p), dpiece(z2, 1, p), zr)
        own = reduced(0, p) + z2[0, at, :].astype(F32) + z2[1, at, :].astype(F32)
        gd_ref[at, :] = own.astype(BF)
        store(gd_ref.at[at, :], gd_hbm.at[at, :])

    for cp in started:
        cp.wait_send()
    for cp in stores:
        cp.wait()
    assert len(names) <= N_SEM and len(stores) <= 16, (len(names), len(stores))


def shards(x_rows, grad_out, gate_pre, up_pre, down_weight):
    rows, width = x_rows.shape
    n_tok, ffl = gate_pre.shape
    kc = down_weight.shape[1]
    hf = ffl // 2
    total = float(rows * lax.axis_size("tensor") * lax.axis_size("dp"))
    gr = kc // 16
    hbm = pl.BlockSpec(memory_space=pl.ANY)

    def kern(*refs):
        kernel(total, *refs)

    outs = [
        ((n_tok, ffl), BF),
        ((n_tok, ffl), BF),
        ((ffl, kc), BF),
        ((gr, BLOCK), F32),
        ((gr, BLOCK), F32),
    ]
    return pl.pallas_call(
        kern,
        out_shape=tuple(jax.ShapeDtypeStruct(*o) for o in outs),
        in_specs=[hbm] * 5,
        out_specs=(hbm,) * 5,
        scratch_shapes=[
            pltpu.VMEM((rows, width), BF),
            pltpu.VMEM((rows, width), BF),
            pltpu.VMEM((n_tok, ffl), BF),
            pltpu.VMEM((n_tok, ffl), BF),
            pltpu.VMEM((ffl, kc), BF),
            *(pltpu.VMEM(*o) for o in outs),
            pltpu.VMEM((rows, kc * 8), BF),
            pltpu.VMEM((2, 4, 2, 2, rows, kc * 8), BF),
            pltpu.VMEM((8, kc, SPLIT), BF),
            pltpu.VMEM((8, kc, ffl - SPLIT), BF),
            pltpu.VMEM((2, ffl, n_tok), BF),
            pltpu.VMEM((2, 2, 4, rows, BLOCK), BF),
            pltpu.VMEM((2, 2, 4, rows, 2 * kc), BF),
            pltpu.VMEM((2, 2, 4, rows, BLOCK), BF),
            pltpu.VMEM((4, ffl, kc), BF),
            pltpu.VMEM((4, ffl, kc), BF),
            pltpu.VMEM((4, ffl, kc), F32),
            pltpu.VMEM((6, hf, kc), BF),
            pltpu.VMEM((2, hf, kc), BF),
            pltpu.VMEM((2, ffl, kc), BF),
            pltpu.VMEM((n_tok, SPLIT), BF),
            pltpu.VMEM((n_tok, ffl - SPLIT), BF),
            pltpu.VMEM((n_tok, SPLIT), BF),
            pltpu.VMEM((n_tok, ffl - SPLIT), BF),
            pltpu.VMEM((n_tok, ffl), F32),
            pltpu.VMEM((2, 4, 4, gr, BLOCK), F32),
            pltpu.VMEM((2, 2, 4, gr, BLOCK), BF),
            pltpu.VMEM((2, 2, 4, gr, BLOCK), BF),
            pltpu.VMEM((2, 4, gr, BLOCK), BF),
            pltpu.VMEM((2, 4, gr, BLOCK), BF),
            pltpu.VMEM((2, 4, gr, BLOCK), F32),
            pltpu.VMEM((2, 3, gr, BLOCK), BF),
            pltpu.VMEM((2, gr, BLOCK), BF),
            pltpu.VMEM((2, 2, gr, BLOCK), BF),
            pltpu.SemaphoreType.DMA((N_SEM,)),
            pltpu.SemaphoreType.DMA((N_SEM,)),
            pltpu.SemaphoreType.DMA((5,)),
            pltpu.SemaphoreType.DMA((16,)),
        ],
        compiler_params=pltpu.CompilerParams(
            collective_id=0, has_side_effects=True, vmem_limit_bytes=60 * 1024 * 1024
        ),
        cost_estimate=pl.CostEstimate(
            flops=4 * n_tok * width * ffl, bytes_accessed=8 * n_tok * ffl, transcendentals=0
        ),
    )(x_rows, grad_out, gate_pre, up_pre, down_weight)


def solution(mesh):
    return jax.shard_map(
        shards,
        mesh=mesh,
        in_specs=(
            P(("dp", "tensor"), None),
            P(("dp", "tensor"), None),
            P("dp", "tensor"),
            P("dp", "tensor"),
            P("tensor", "dp"),
        ),
        out_specs=(
            P("dp", "tensor"),
            P("dp", "tensor"),
            P("tensor", "dp"),
            P(("tensor", "dp"), None),
            P(("tensor", "dp"), None),
        ),
        check_vma=False,
    )
```

```python
import math

import jax
import jax.numpy as jnp
from jax import lax
from jax.experimental import pallas as pl
from jax.experimental.pallas import tpu as pltpu
from jax.sharding import PartitionSpec as P

MESH = pl.DeviceIdType.MESH
BF = jnp.bfloat16
F32 = jnp.float32
BLOCK = 1024
N_SEM = 128
SPLIT = 512
FIRST = 128


def kernel(
    total,
    x_hbm, g_hbm, gate_hbm, up_hbm, w_hbm,
    gg_hbm, gu_hbm, gd_hbm, gi_hbm, go_hbm,
    x_ref, g_ref, gate_ref, up_ref, w_ref,
    gg_ref, gu_ref, gd_ref, gi_ref, go_ref,
    ghalf, tok, wf0, wf1, ht, xi, xo_buf, gm, asnd, arcv, part, zs, z1, z2,
    fp, fs1, fs2, f1, f2, fas, far,
    snd0, snd1, rcv0, rcv1, ghf, gp, gbs, gbr, gas, gar, gf, gzs, gz1, gz2,
    ssem, rsem, isem, osem,
):
    rows = g_ref.shape[0]
    ffl, kc = w_ref.shape
    n_tok = gate_ref.shape[0]
    hk = kc // 2
    hd = ffl - FIRST
    hf = hd // 2
    hcols = (pl.ds(0, SPLIT), pl.ds(SPLIT, ffl - SPLIT))
    d = lax.axis_index("dp")
    t = lax.axis_index("tensor")
    zh, y = d // 4, d % 4
    x, zl, c = t // 4, (t // 2) % 2, t % 2
    half = ((y + 1) // 2) % 2
    s = y // 2

    sib = (d, t + 1 - 2 * c)
    zlp = (d, t + 2 - 4 * zl)
    xr = (d, ((x + 1) % 4) * 4 + t % 4)
    xl = (d, ((x + 3) % 4) * 4 + t % 4)
    xo = (d, ((x + 2) % 4) * 4 + t % 4)
    ya = (zh * 4 + 3 - y, t)
    yb = (zh * 4 + y + 1 - 2 * (y % 2), t)
    zr = (((zh + 1) % 4) * 4 + y, t)
    zb = (((zh + 3) % 4) * 4 + y, t)
    zo = (((zh + 3 + 2 * zl) % 4) * 4 + y, t + 2 - 4 * zl)
    neighbours = (sib, zlp, zo, xr, xl, xo, ya, yb, zr, zb)

    barrier = pltpu.get_barrier_semaphore()
    for n in neighbours:
        pl.semaphore_signal(barrier, inc=1, device_id=n, device_id_type=MESH)
    loads = [
        pltpu.make_async_copy(a, b, isem.at[i])
        for i, (a, b) in enumerate(
            ((w_hbm, w_ref), (g_hbm, g_ref), (gate_hbm, gate_ref), (up_hbm, up_ref), (x_hbm, x_ref))
        )
    ]
    for cp in loads:
        cp.start()

    names = {}
    started = []
    stores = []

    def sem(key):
        return names.setdefault(key, len(names))

    def send(key, src_ref, dst_ref, dev):
        k = sem(key)
        cp = pltpu.make_async_remote_copy(
            src_ref=src_ref, dst_ref=dst_ref, send_sem=ssem.at[k], recv_sem=rsem.at[k],
            device_id=dev, device_id_type=MESH,
        )
        cp.start()
        started.append(cp)

    def recv(key, dst_ref, dev):
        k = sem(key)
        pltpu.make_async_remote_copy(
            src_ref=dst_ref, dst_ref=dst_ref, send_sem=ssem.at[k], recv_sem=rsem.at[k],
            device_id=dev, device_id_type=MESH,
        ).wait_recv()

    def store(src_ref, dst_ref):
        cp = pltpu.make_async_copy(src_ref, dst_ref, osem.at[len(stores)])
        cp.start()
        stores.append(cp)

    def zz(r):
        return (zh + r) % 4

    def yy_of(h, q):
        return h + q * (3 - 2 * h)

    def wpiece(r, q, hh, kh=None):
        ref = (wf0, wf1)[hh]
        if kh is None:
            return ref.at[zz(r) * 2 + q]
        return ref.at[zz(r) * 2 + q, pl.ds(kh * hk, hk), :]

    def w_to_a(r, hh, kh=None):
        send(("wa", r, hh, kh), wpiece(r, s, hh, kh), wpiece(r, s, hh, kh), ya)

    def w_own(hh, i):
        send(("wl", hh, i), wpiece(0, s, hh, i), wpiece(0, s, hh, i), zr)
        send(("wr", hh, i), wpiece(0, s, hh, 1 - i), wpiece(0, s, hh, 1 - i), zb)

    def w_mid(hh, i):
        recv(("wl", hh, i), wpiece(3, s, hh, i), zb)
        if i == 0:
            send(("wo", hh, 0), wpiece(3, s, hh, 0), wpiece(3, s, hh, 0), zr)
        recv(("wr", hh, i), wpiece(1, s, hh, 1 - i), zr)
        if i == 0:
            send(("wo", hh, 1), wpiece(1, s, hh, 1), wpiece(1, s, hh, 1), zb)
        w_to_a(3, hh, i)
        w_to_a(1, hh, 1 - i)

    def w_opp(hh, kh):
        recv(("wo", hh, kh), wpiece(2, s, hh, kh), zb if kh == 0 else zr)
        w_to_a(2, hh, kh)

    def w_from_a(hh):
        recv(("wa", 0, hh, None), wpiece(0, 1 - s, hh), ya)
        for r in (3, 1, 2):
            for kh in range(2):
                recv(("wa", r, hh, kh), wpiece(r, 1 - s, hh, kh), ya)

    loads[0].wait()
    wf0[zh * 2 + s] = w_ref[:SPLIT, :].astype(F32).T.astype(BF)
    wf1[zh * 2 + s] = w_ref[SPLIT:, :].astype(F32).T.astype(BF)

    loads[1].wait()
    for z in range(4):
        for q in range(2):
            to = pl.ds((z * 2 + q) * kc, kc)
            other = pl.multiple_of((z * 4 + yy_of(1 - half, q)) * kc, kc)
            mine = pl.multiple_of((z * 4 + yy_of(half, q)) * kc, kc)
            ghalf[:, to] = g_ref[:, pl.ds(other, kc)]
            tok[0, x, zl, c, :, to] = g_ref[:, pl.ds(mine, kc)]

    pl.semaphore_wait(barrier, len(neighbours))

    w_to_a(0, 0)
    w_own(0, 0)
    w_own(0, 1)

    def tpiece(slot, e, xx, cc=c):
        return tok.at[slot, xx, zl if e == 0 else 1 - zl, cc]

    x_left, x_right, x_opp = (x + 3) % 4, (x + 1) % 4, (x + 2) % 4

    def t_to_x(slot, e):
        ref = tpiece(slot, e, x)
        send(("txl", slot, e), ref, ref, xr)
        send(("txr", slot, e), ref, ref, xl)
        send(("ts", slot, e, 0), ref, ref, sib)

    wide = kc * 4

    def thalf(ref, p):
        return ref.at[:, pl.ds(p * wide, wide)]

    def t_from_x(slot, e):
        left, right = tpiece(slot, e, x_left), tpiece(slot, e, x_right)
        recv(("txl", slot, e), left, xl)
        send(("txo", slot, e, 0), thalf(left, 0), thalf(left, 0), xr)
        send(("ts", slot, e, 3), left, left, sib)
        recv(("txr", slot, e), right, xr)
        send(("txo", slot, e, 1), thalf(right, 1), thalf(right, 1), xl)
        send(("ts", slot, e, 1), right, right, sib)

    def t_from_opp(slot, e):
        opp = tpiece(slot, e, x_opp)
        recv(("txo", slot, e, 0), thalf(opp, 0), xl)
        recv(("txo", slot, e, 1), thalf(opp, 1), xr)
        send(("ts", slot, e, 2), opp, opp, sib)

    def t_to_z(slot):
        send(("tz", slot), tpiece(slot, 0, x), tpiece(slot, 0, x), zlp)

    send("tb", ghalf, tok.at[1, x, zl, c], yb)
    t_to_x(0, 0)
    w_to_a(0, 1)

    loads[2].wait()
    loads[3].wait()
    ht_tile = 128

    def hidden_tile(i):
        at = pl.ds(pl.multiple_of(i * ht_tile, ht_tile), ht_tile)
        gate = gate_ref[at, :].astype(F32)
        up = up_ref[at, :].astype(F32)
        hid = (gate * jax.nn.sigmoid(gate) * up).astype(BF)
        ht[0, :, at] = hid.astype(F32).T.astype(BF)

    n_ht = n_tok // ht_tile
    for p in range(2):
        pl.loop(p * n_ht // 2, (p + 1) * n_ht // 2)(hidden_tile)
        cols = pl.ds(p * n_tok // 2, n_tok // 2)
        send(("h", p), ht.at[0, :, cols], ht.at[1, :, cols], yb)

    loads[4].wait()

    def x_cols(xx):
        return pl.ds(pl.multiple_of(xx * BLOCK, BLOCK), BLOCK)

    def o_cols(xx):
        return pl.ds(pl.multiple_of(xx * 2 * kc, 2 * kc), 2 * kc)

    xi[c, zl, x] = x_ref[:, x_cols(x)]
    xo_buf[c, zl, x] = ghalf[:, o_cols(x)]
    for r, dev in ((1, xr), (3, xl), (2, xo)):
        send(("gxi", r), x_ref.at[:, x_cols((x + r) % 4)], xi.at[c, zl, x], dev)
        send(("gxo", r), ghalf.at[:, o_cols((x + r) % 4)], xo_buf.at[c, zl, x], dev)

    def gram_cols():
        for r, dev in ((3, xr), (1, xl), (2, xo)):
            recv(("gxi", r), xi.at[c, zl, (x + 4 - r) % 4], dev)
        send("gzi", xi.at[c, zl], xi.at[c, zl], zo)

    def gram_in_sib():
        recv("gzi", xi.at[c, 1 - zl], zo)
        send("gsi", xi.at[c], xi.at[c], sib)

    def tz_in(slot):
        recv(("tz", slot), tpiece(slot, 1, x), zlp)
        t_to_x(slot, 1)

    recv("tb", tpiece(1, 0, x), yb)
    t_to_x(1, 0)
    w_mid(0, 0)
    t_from_x(0, 0)
    w_mid(0, 1)
    t_to_z(0)
    t_to_z(1)
    gram_cols()
    t_from_x(1, 0)
    w_opp(0, 0)
    w_opp(0, 1)
    w_own(1, 0)
    tz_in(0)
    tz_in(1)
    w_own(1, 1)
    t_from_x(0, 1)
    w_mid(1, 0)
    t_from_x(1, 1)
    gram_in_sib()

    my_cols = pl.ds(pl.multiple_of((zl * 2 + c) * kc, kc), kc)

    def gram(a, ref):
        lhs, rhs = ref[:, :, :, :, my_cols].reshape(n_tok, kc), ref[...].reshape(n_tok, BLOCK)
        out = lax.dot_general(lhs, rhs, (((0,), (0,)), ((), ())), preferred_element_type=F32)
        for z in range(4):
            for q in range(4):
                gp[a, q, z] = out[(z * 4 + q) * 16:(z * 4 + q + 1) * 16, :]
        for q in range(2):
            gbs[a, q] = gp[a, yy_of(1 - half, q)].astype(BF)

    w_mid(1, 1)
    t_from_opp(0, 0)
    t_from_opp(1, 0)
    t_from_opp(0, 1)
    t_from_opp(1, 1)
    w_opp(1, 0)
    w_opp(1, 1)
    recv("gsi", xi.at[1 - c], sib)
    gram(0, xi)
    for r, dev in ((3, xr), (1, xl), (2, xo)):
        recv(("gxo", r), xo_buf.at[c, zl, (x + 4 - r) % 4], dev)
    send("gzo", xo_buf.at[c, zl], xo_buf.at[c, zl], zlp)
    for p in range(2):
        cols = pl.ds(p * n_tok // 2, n_tok // 2)
        recv(("h", p), ht.at[1, :, cols], yb)
    send(("gb", 0), gbs.at[0], gbr.at[0], yb)

    for slot in range(2):
        for e in range(2):
            for r in range(4):
                recv(("ts", slot, e, r), tpiece(slot, e, (x + r) % 4, 1 - c), sib)

    scale = 1.0 / math.sqrt(total)

    def down(r, q):
        cols = pl.ds(pl.multiple_of((zz(r) * 2 + q) * kc, kc), kc)
        acc = jnp.dot(ht[0, :hd, :], tok[0, :, :, :, :, cols].reshape(n_tok, kc), preferred_element_type=F32)
        acc += jnp.dot(ht[1, :hd, :], tok[1, :, :, :, :, cols].reshape(n_tok, kc), preferred_element_type=F32)
        return acc * scale

    def dpiece(ref, i, p):
        return ref.at[i, pl.ds(p * hf, hf), :]

    def down_to_a(r, p):
        send(("da", r, p), dpiece(asnd, r, p), dpiece(arcv, r, p), ya)

    def first_rows():
        acc = jnp.dot(ht[0, hd:, :], tok[0].reshape(n_tok, kc * 8), preferred_element_type=F32)
        acc += jnp.dot(ht[1, hd:, :], tok[1].reshape(n_tok, kc * 8), preferred_element_type=F32)
        for j in range(8):
            fp[j] = acc[:, j * kc:(j + 1) * kc] * scale
        for q in range(2):
            fs1[q] = fp[zz(2) * 2 + q].astype(BF)
            send(("f1", q), fs1.at[q], f1.at[q], zr if q == 0 else zb)

    def first_rows_2():
        for q in range(2):
            recv(("f1", q), f1.at[q], zb if q == 0 else zr)
            r = 1 if q == 0 else 3
            fs2[q, q] = (fp[zz(r) * 2 + q] + f1[q].astype(F32)).astype(BF)
            fs2[q, 1 - q] = fp[zz(r) * 2 + 1 - q].astype(BF)
            send(("f2", q), fs2.at[q], f2.at[q], zr if q == 0 else zb)

    def first_sum(q):
        return fp[zh * 2 + q] + f2[0, q].astype(F32) + f2[1, q].astype(F32)

    def first_rows_to_a():
        recv(("f2", 0), f2.at[0], zb)
        recv(("f2", 1), f2.at[1], zr)
        fas[...] = first_sum(1 - s).astype(BF)
        send("fa", fas, far, ya)

    n_tile = n_tok // 2

    def hidden_grad(slot, hh, i):
        lhs = tok[slot, 2 * i:2 * i + 2].reshape(n_tile, kc * 8)
        rhs = wf0[...].reshape(kc * 8, SPLIT) if hh == 0 else wf1[...].reshape(kc * 8, ffl - SPLIT)
        return jnp.dot(lhs, rhs, preferred_element_type=F32)

    def hidden_to_b(hh, i):
        at = pl.ds(i * n_tile, n_tile)
        snd, rcv = (snd0, snd1)[hh], (rcv0, rcv1)[hh]
        send(("gh", hh, i), snd.at[at, :], rcv.at[at, :], yb)

    asnd[2] = down(2, 1 - s).astype(BF)
    down_to_a(2, 0)
    down_to_a(2, 1)
    first_rows()
    w_from_a(0)
    for i in range(2):
        snd0[i * n_tile:(i + 1) * n_tile, :] = hidden_grad(1, 0, i).astype(BF)
        hidden_to_b(0, i)
    asnd[1] = down(1, 1 - s).astype(BF)
    asnd[3] = down(3, 1 - s).astype(BF)
    part[2] = down(2, s)
    first_rows_2()
    w_from_a(1)
    for i in range(2):
        snd1[i * n_tile:(i + 1) * n_tile, :] = hidden_grad(1, 1, i).astype(BF)

    def reduced(r, p):
        recv(("da", r, p), dpiece(arcv, r, p), ya)
        at = pl.ds(p * hf, hf)
        return part[r, at, :] + arcv[r, at, :].astype(F32)

    def gram_to_a(a):
        recv(("gb", a), gbr.at[a], yb)
        gas[a] = (gp[a, yy_of(half, 1 - s)] + gbr[a, 1 - s].astype(F32)).astype(BF)
        send(("ga", a), gas.at[a], gar.at[a], ya)
        gf[a] = gp[a, yy_of(half, s)] + gbr[a, s].astype(F32)

    def gram_z1(a):
        recv(("ga", a), gar.at[a], ya)
        gf[a] = gf[a] + gar[a].astype(F32)
        gzs[a, 0] = gf[a, zz(2)].astype(BF)
        send(("gz1", a), gzs.at[a, 0], gz1.at[a], zr if a == 0 else zb)

    def gram_z2(a):
        recv(("gz1", a), gz1.at[a], zb if a == 0 else zr)
        passed = gz1[a].astype(F32)
        gzs[a, 1] = (gf[a, zz(1)] + passed if a == 0 else gf[a, zz(1)]).astype(BF)
        send(("gz2r", a), gzs.at[a, 1], gz2.at[a, 0], zr)
        gzs[a, 2] = (gf[a, zz(3)] + passed if a == 1 else gf[a, zz(3)]).astype(BF)
        send(("gz2l", a), gzs.at[a, 2], gz2.at[a, 1], zb)

    def gram_out(a, out, hbm):
        recv(("gz2r", a), gz2.at[a, 0], zb)
        recv(("gz2l", a), gz2.at[a, 1], zr)
        out[...] = (gf[a, zh] + gz2[a, 0].astype(F32) + gz2[a, 1].astype(F32)) / total
        store(out, hbm)

    gram_to_a(0)
    recv("gzo", xo_buf.at[c, 1 - zl], zlp)
    send("gso", xo_buf.at[c], xo_buf.at[c], sib)
    for q in range(2):
        mine = pl.ds(pl.multiple_of(yy_of(half, q) * kc, kc), kc)
        from_tok = pl.ds(pl.multiple_of((x * 2 + q) * kc, kc), kc)
        for cc in range(2):
            for zc in range(2):
                for xc in range(4):
                    gm[cc, zc, xc, :, mine] = tok[0, xc, zc, cc, :, from_tok]
    recv("gso", xo_buf.at[1 - c], sib)
    for q in range(2):
        other = pl.ds(pl.multiple_of(yy_of(1 - half, q) * kc, kc), kc)
        gm[:, :, :, :, other] = xo_buf[:, :, :, :, q * kc:(q + 1) * kc]
    gram(1, gm)
    send(("gb", 1), gbs.at[1], gbr.at[1], yb)
    hidden_to_b(1, 0)
    hidden_to_b(1, 1)

    zs[0] = reduced(2, 0).astype(BF)
    send(("z1", 0), zs.at[0], z1.at[0], zr)
    down_to_a(1, 1)
    down_to_a(3, 0)
    zs[1] = reduced(2, 1).astype(BF)
    send(("z1", 1), zs.at[1], z1.at[1], zb)
    down_to_a(1, 0)
    down_to_a(3, 1)
    first_rows_to_a()
    gram_z1(0)
    part[1] = down(1, s)
    part[3] = down(3, s)
    asnd[0] = down(0, 1 - s).astype(BF)
    gram_z2(0)
    gram_to_a(1)
    zs[2] = reduced(1, 1).astype(BF)
    send(("z2r", 1), zs.at[2], dpiece(z2, 0, 1), zr)
    zs[3] = reduced(3, 0).astype(BF)
    send(("z2l", 0), zs.at[3], dpiece(z2, 1, 0), zb)
    down_to_a(0, 0)
    down_to_a(0, 1)
    gram_z1(1)

    recv(("z1", 0), z1.at[0], zb)
    zs[4] = (reduced(1, 0) + z1[0].astype(F32)).astype(BF)
    send(("z2r", 0), zs.at[4], dpiece(z2, 0, 0), zr)
    recv(("z1", 1), z1.at[1], zr)
    zs[5] = (reduced(3, 1) + z1[1].astype(F32)).astype(BF)
    send(("z2l", 1), zs.at[5], dpiece(z2, 1, 1), zb)

    part[0] = down(0, s)
    for hh in range(2):
        for i in range(2):
            ghf[i * n_tile:(i + 1) * n_tile, hcols[hh]] = hidden_grad(0, hh, i)

    step = 32

    def finish(hh):
        rcv, cols = (rcv0, rcv1)[hh], hcols[hh]
        for i in range(2):
            at = pl.ds(i * n_tile, n_tile)
            recv(("gh", hh, i), rcv.at[at, :], yb)

            @pl.loop(0, n_tile // step)
            def _(k):
                rows_at = pl.ds(pl.multiple_of(i * n_tile + k * step, step), step)
                gh = ghf[rows_at, cols] + rcv[rows_at, :].astype(F32)
                gate = gate_ref[rows_at, cols].astype(F32)
                up = up_ref[rows_at, cols].astype(F32)
                sigma = jax.nn.sigmoid(gate)
                gu_ref[rows_at, cols] = (gh * (gate * sigma)).astype(BF)
                gg_ref[rows_at, cols] = (gh * up * sigma * (1.0 + gate * (1.0 - sigma))).astype(BF)

            store(gu_ref.at[at, cols], gu_hbm.at[at, cols])
            store(gg_ref.at[at, cols], gg_hbm.at[at, cols])

    finish(0)

    gram_z2(1)
    gram_out(0, gi_ref, gi_hbm)
    finish(1)
    gram_out(1, go_ref, go_hbm)

    last = pl.ds(hd, FIRST)
    recv("fa", far, ya)
    gd_ref[last, :] = (first_sum(s) + far[...].astype(F32)).astype(BF)
    store(gd_ref.at[last, :], gd_hbm.at[last, :])

    for p in range(2):
        at = pl.ds(p * hf, hf)
        recv(("z2r", p), dpiece(z2, 0, p), zb)
        recv(("z2l", p), dpiece(z2, 1, p), zr)
        own = reduced(0, p) + z2[0, at, :].astype(F32) + z2[1, at, :].astype(F32)
        gd_ref[at, :] = own.astype(BF)
        store(gd_ref.at[at, :], gd_hbm.at[at, :])

    for cp in started:
        cp.wait_send()
    for cp in stores:
        cp.wait()
    assert len(names) <= N_SEM and len(stores) <= 16, (len(names), len(stores))


PARTS = 4


def hand_over(*refs):
    ins, outs = [], []
    for i in range(5):
        src, dst, mid = refs[i], refs[5 + i], refs[10 + i]
        parts = PARTS if i < 3 else 1
        n = src.shape[0] // parts
        for p in range(parts):
            at = pl.ds(p * n, n)
            ins.append(pltpu.make_async_copy(src.at[at, :], mid.at[at, :], refs[15].at[i, p]))
            outs.append(pltpu.make_async_copy(mid.at[at, :], dst.at[at, :], refs[16].at[i, p]))
    for cp in ins:
        cp.start()
    for cp, out in zip(ins, outs):
        cp.wait()
        out.start()
    for cp in outs:
        cp.wait()


def shards(x_rows, grad_out, gate_pre, up_pre, down_weight):
    rows, width = x_rows.shape
    n_tok, ffl = gate_pre.shape
    kc = down_weight.shape[1]
    hd = ffl - FIRST
    hf = hd // 2
    total = float(rows * lax.axis_size("tensor") * lax.axis_size("dp"))
    gr = kc // 16
    hbm = pl.BlockSpec(memory_space=pl.ANY)

    def kern(*refs):
        kernel(total, *refs)

    outs = [
        ((n_tok, ffl), BF),
        ((n_tok, ffl), BF),
        ((ffl, kc), BF),
        ((gr, BLOCK), F32),
        ((gr, BLOCK), F32),
    ]
    results = pl.pallas_call(
        kern,
        out_shape=tuple(jax.ShapeDtypeStruct(*o) for o in outs),
        in_specs=[hbm] * 5,
        out_specs=(hbm,) * 5,
        scratch_shapes=[
            pltpu.VMEM((rows, width), BF),
            pltpu.VMEM((rows, width), BF),
            pltpu.VMEM((n_tok, ffl), BF),
            pltpu.VMEM((n_tok, ffl), BF),
            pltpu.VMEM((ffl, kc), BF),
            *(pltpu.VMEM(*o) for o in outs),
            pltpu.VMEM((rows, kc * 8), BF),
            pltpu.VMEM((2, 4, 2, 2, rows, kc * 8), BF),
            pltpu.VMEM((8, kc, SPLIT), BF),
            pltpu.VMEM((8, kc, ffl - SPLIT), BF),
            pltpu.VMEM((2, ffl, n_tok), BF),
            pltpu.VMEM((2, 2, 4, rows, BLOCK), BF),
            pltpu.VMEM((2, 2, 4, rows, 2 * kc), BF),
            pltpu.VMEM((2, 2, 4, rows, BLOCK), BF),
            pltpu.VMEM((4, hd, kc), BF),
            pltpu.VMEM((4, hd, kc), BF),
            pltpu.VMEM((4, hd, kc), F32),
            pltpu.VMEM((6, hf, kc), BF),
            pltpu.VMEM((2, hf, kc), BF),
            pltpu.VMEM((2, hd, kc), BF),
            pltpu.VMEM((8, FIRST, kc), F32),
            pltpu.VMEM((2, FIRST, kc), BF),
            pltpu.VMEM((2, 2, FIRST, kc), BF),
            pltpu.VMEM((2, FIRST, kc), BF),
            pltpu.VMEM((2, 2, FIRST, kc), BF),
            pltpu.VMEM((FIRST, kc), BF),
            pltpu.VMEM((FIRST, kc), BF),
            pltpu.VMEM((n_tok, SPLIT), BF),
            pltpu.VMEM((n_tok, ffl - SPLIT), BF),
            pltpu.VMEM((n_tok, SPLIT), BF),
            pltpu.VMEM((n_tok, ffl - SPLIT), BF),
            pltpu.VMEM((n_tok, ffl), F32),
            pltpu.VMEM((2, 4, 4, gr, BLOCK), F32),
            pltpu.VMEM((2, 2, 4, gr, BLOCK), BF),
            pltpu.VMEM((2, 2, 4, gr, BLOCK), BF),
            pltpu.VMEM((2, 4, gr, BLOCK), BF),
            pltpu.VMEM((2, 4, gr, BLOCK), BF),
            pltpu.VMEM((2, 4, gr, BLOCK), F32),
            pltpu.VMEM((2, 3, gr, BLOCK), BF),
            pltpu.VMEM((2, gr, BLOCK), BF),
            pltpu.VMEM((2, 2, gr, BLOCK), BF),
            pltpu.SemaphoreType.DMA((N_SEM,)),
            pltpu.SemaphoreType.DMA((N_SEM,)),
            pltpu.SemaphoreType.DMA((5,)),
            pltpu.SemaphoreType.DMA((16,)),
        ],
        compiler_params=pltpu.CompilerParams(
            collective_id=0, has_side_effects=True, vmem_limit_bytes=60 * 1024 * 1024
        ),
        cost_estimate=pl.CostEstimate(
            flops=4 * n_tok * width * ffl, bytes_accessed=8 * n_tok * ffl, transcendentals=0
        ),
    )(x_rows, grad_out, gate_pre, up_pre, down_weight)
    return pl.pallas_call(
        hand_over,
        out_shape=tuple(jax.ShapeDtypeStruct(*o) for o in outs),
        in_specs=[hbm] * 5,
        out_specs=(hbm,) * 5,
        scratch_shapes=[
            *(pltpu.VMEM(*o) for o in outs),
            pltpu.SemaphoreType.DMA((5, PARTS)),
            pltpu.SemaphoreType.DMA((5, PARTS)),
        ],
        compiler_params=pltpu.CompilerParams(vmem_limit_bytes=60 * 1024 * 1024),
    )(*results)


def solution(mesh):
    return jax.shard_map(
        shards,
        mesh=mesh,
        in_specs=(
            P(("dp", "tensor"), None),
            P(("dp", "tensor"), None),
            P("dp", "tensor"),
            P("dp", "tensor"),
            P("tensor", "dp"),
        ),
        out_specs=(
            P("dp", "tensor"),
            P("dp", "tensor"),
            P("tensor", "dp"),
            P(("tensor", "dp"), None),
            P(("tensor", "dp"), None),
        ),
        check_vma=False,
    )
```

```python
import math

import jax
import jax.numpy as jnp
from jax import lax
from jax.experimental import pallas as pl
from jax.experimental.pallas import tpu as pltpu
from jax.sharding import PartitionSpec as P

MESH = pl.DeviceIdType.MESH
BF = jnp.bfloat16
F32 = jnp.float32
BLOCK = 1024
N_SEM = 128
SPLIT = 512
FIRST = 160


def kernel(
    total,
    x_hbm, g_hbm, gate_hbm, up_hbm, w_hbm,
    gg_hbm, gu_hbm, gd_hbm, gi_hbm, go_hbm,
    x_ref, g_ref, gate_ref, up_ref, w_ref,
    gg_ref, gu_ref, gd_ref, gi_ref, go_ref,
    ghalf, tok, wf0, wf1, ht, xi, xo_buf, gm, asnd, arcv, part, zs, z1, z2,
    fp, fs1, fs2, f1, f2, fas, far,
    snd0, snd1, rcv0, rcv1, ghf, gp, gbs, gbr, gas, gar, gf, gzs, gz1, gz2,
    ssem, rsem, isem, osem,
):
    rows = g_ref.shape[0]
    ffl, kc = w_ref.shape
    n_tok = gate_ref.shape[0]
    hk = kc // 2
    hd = ffl - FIRST
    hf = hd // 2
    hcols = (pl.ds(0, SPLIT), pl.ds(SPLIT, ffl - SPLIT))
    d = lax.axis_index("dp")
    t = lax.axis_index("tensor")
    zh, y = d // 4, d % 4
    x, zl, c = t // 4, (t // 2) % 2, t % 2
    half = ((y + 1) // 2) % 2
    s = y // 2

    sib = (d, t + 1 - 2 * c)
    zlp = (d, t + 2 - 4 * zl)
    xr = (d, ((x + 1) % 4) * 4 + t % 4)
    xl = (d, ((x + 3) % 4) * 4 + t % 4)
    xo = (d, ((x + 2) % 4) * 4 + t % 4)
    ya = (zh * 4 + 3 - y, t)
    yb = (zh * 4 + y + 1 - 2 * (y % 2), t)
    zr = (((zh + 1) % 4) * 4 + y, t)
    zb = (((zh + 3) % 4) * 4 + y, t)
    zo = (((zh + 3 + 2 * zl) % 4) * 4 + y, t + 2 - 4 * zl)
    neighbours = (sib, zlp, zo, xr, xl, xo, ya, yb, zr, zb)

    barrier = pltpu.get_barrier_semaphore()
    for n in neighbours:
        pl.semaphore_signal(barrier, inc=1, device_id=n, device_id_type=MESH)
    loads = [
        pltpu.make_async_copy(a, b, isem.at[i])
        for i, (a, b) in enumerate(
            ((w_hbm, w_ref), (g_hbm, g_ref), (gate_hbm, gate_ref), (up_hbm, up_ref), (x_hbm, x_ref))
        )
    ]
    for cp in loads:
        cp.start()

    names = {}
    started = []
    stores = []

    def sem(key):
        return names.setdefault(key, len(names))

    def send(key, src_ref, dst_ref, dev):
        k = sem(key)
        cp = pltpu.make_async_remote_copy(
            src_ref=src_ref, dst_ref=dst_ref, send_sem=ssem.at[k], recv_sem=rsem.at[k],
            device_id=dev, device_id_type=MESH,
        )
        cp.start()
        started.append(cp)

    def recv(key, dst_ref, dev):
        k = sem(key)
        pltpu.make_async_remote_copy(
            src_ref=dst_ref, dst_ref=dst_ref, send_sem=ssem.at[k], recv_sem=rsem.at[k],
            device_id=dev, device_id_type=MESH,
        ).wait_recv()

    def store(src_ref, dst_ref):
        cp = pltpu.make_async_copy(src_ref, dst_ref, osem.at[len(stores)])
        cp.start()
        stores.append(cp)

    def zz(r):
        return (zh + r) % 4

    def yy_of(h, q):
        return h + q * (3 - 2 * h)

    def wpiece(r, q, hh, kh=None):
        ref = (wf0, wf1)[hh]
        if kh is None:
            return ref.at[zz(r) * 2 + q]
        return ref.at[zz(r) * 2 + q, pl.ds(kh * hk, hk), :]

    def w_to_a(r, hh, kh=None):
        send(("wa", r, hh, kh), wpiece(r, s, hh, kh), wpiece(r, s, hh, kh), ya)

    def w_own(hh, i):
        send(("wl", hh, i), wpiece(0, s, hh, i), wpiece(0, s, hh, i), zr)
        send(("wr", hh, i), wpiece(0, s, hh, 1 - i), wpiece(0, s, hh, 1 - i), zb)

    def w_mid(hh, i):
        recv(("wl", hh, i), wpiece(3, s, hh, i), zb)
        if i == 0:
            send(("wo", hh, 0), wpiece(3, s, hh, 0), wpiece(3, s, hh, 0), zr)
        recv(("wr", hh, i), wpiece(1, s, hh, 1 - i), zr)
        if i == 0:
            send(("wo", hh, 1), wpiece(1, s, hh, 1), wpiece(1, s, hh, 1), zb)
        w_to_a(3, hh, i)
        w_to_a(1, hh, 1 - i)

    def w_opp(hh, kh):
        recv(("wo", hh, kh), wpiece(2, s, hh, kh), zb if kh == 0 else zr)
        w_to_a(2, hh, kh)

    def w_from_a(hh):
        recv(("wa", 0, hh, None), wpiece(0, 1 - s, hh), ya)
        for r in (3, 1, 2):
            for kh in range(2):
                recv(("wa", r, hh, kh), wpiece(r, 1 - s, hh, kh), ya)

    loads[0].wait()
    wf0[zh * 2 + s] = w_ref[:SPLIT, :].astype(F32).T.astype(BF)
    wf1[zh * 2 + s] = w_ref[SPLIT:, :].astype(F32).T.astype(BF)

    loads[1].wait()
    for z in range(4):
        for q in range(2):
            to = pl.ds((z * 2 + q) * kc, kc)
            other = pl.multiple_of((z * 4 + yy_of(1 - half, q)) * kc, kc)
            mine = pl.multiple_of((z * 4 + yy_of(half, q)) * kc, kc)
            ghalf[:, to] = g_ref[:, pl.ds(other, kc)]
            tok[0, x, zl, c, :, to] = g_ref[:, pl.ds(mine, kc)]

    pl.semaphore_wait(barrier, len(neighbours))

    w_to_a(0, 0)
    w_own(0, 0)
    w_own(0, 1)

    def tpiece(slot, e, xx, cc=c):
        return tok.at[slot, xx, zl if e == 0 else 1 - zl, cc]

    x_left, x_right, x_opp = (x + 3) % 4, (x + 1) % 4, (x + 2) % 4

    def t_to_x(slot, e):
        ref = tpiece(slot, e, x)
        send(("txl", slot, e), ref, ref, xr)
        send(("txr", slot, e), ref, ref, xl)
        send(("ts", slot, e, 0), ref, ref, sib)

    wide = kc * 4

    def thalf(ref, p):
        return ref.at[:, pl.ds(p * wide, wide)]

    def t_from_x(slot, e):
        left, right = tpiece(slot, e, x_left), tpiece(slot, e, x_right)
        recv(("txl", slot, e), left, xl)
        send(("txo", slot, e, 0), thalf(left, 0), thalf(left, 0), xr)
        send(("ts", slot, e, 3), left, left, sib)
        recv(("txr", slot, e), right, xr)
        send(("txo", slot, e, 1), thalf(right, 1), thalf(right, 1), xl)
        send(("ts", slot, e, 1), right, right, sib)

    def t_from_opp(slot, e):
        opp = tpiece(slot, e, x_opp)
        recv(("txo", slot, e, 0), thalf(opp, 0), xl)
        recv(("txo", slot, e, 1), thalf(opp, 1), xr)
        send(("ts", slot, e, 2), opp, opp, sib)

    def t_to_z(slot):
        send(("tz", slot), tpiece(slot, 0, x), tpiece(slot, 0, x), zlp)

    send("tb", ghalf, tok.at[1, x, zl, c], yb)
    t_to_x(0, 0)
    w_to_a(0, 1)

    loads[2].wait()
    loads[3].wait()
    ht_tile = 128

    def hidden_tile(i):
        at = pl.ds(pl.multiple_of(i * ht_tile, ht_tile), ht_tile)
        gate = gate_ref[at, :].astype(F32)
        up = up_ref[at, :].astype(F32)
        hid = (gate * jax.nn.sigmoid(gate) * up).astype(BF)
        ht[0, :, at] = hid.astype(F32).T.astype(BF)

    n_ht = n_tok // ht_tile
    for p in range(2):
        pl.loop(p * n_ht // 2, (p + 1) * n_ht // 2)(hidden_tile)
        cols = pl.ds(p * n_tok // 2, n_tok // 2)
        send(("h", p), ht.at[0, :, cols], ht.at[1, :, cols], yb)

    loads[4].wait()

    def x_cols(xx):
        return pl.ds(pl.multiple_of(xx * BLOCK, BLOCK), BLOCK)

    def o_cols(xx):
        return pl.ds(pl.multiple_of(xx * 2 * kc, 2 * kc), 2 * kc)

    xi[c, zl, x] = x_ref[:, x_cols(x)]
    xo_buf[c, zl, x] = ghalf[:, o_cols(x)]
    for r, dev in ((1, xr), (3, xl), (2, xo)):
        send(("gxi", r), x_ref.at[:, x_cols((x + r) % 4)], xi.at[c, zl, x], dev)
        send(("gxo", r), ghalf.at[:, o_cols((x + r) % 4)], xo_buf.at[c, zl, x], dev)

    def gram_cols():
        for r, dev in ((3, xr), (1, xl), (2, xo)):
            recv(("gxi", r), xi.at[c, zl, (x + 4 - r) % 4], dev)
        send("gzi", xi.at[c, zl], xi.at[c, zl], zo)

    def gram_in_sib():
        recv("gzi", xi.at[c, 1 - zl], zo)
        send("gsi", xi.at[c], xi.at[c], sib)

    def tz_in(slot):
        recv(("tz", slot), tpiece(slot, 1, x), zlp)
        t_to_x(slot, 1)

    recv("tb", tpiece(1, 0, x), yb)
    t_to_x(1, 0)
    w_mid(0, 0)
    t_from_x(0, 0)
    t_to_z(0)
    w_mid(0, 1)
    t_to_z(1)
    gram_cols()
    t_from_x(1, 0)
    w_opp(0, 0)
    w_opp(0, 1)
    w_own(1, 0)
    tz_in(0)
    tz_in(1)
    w_own(1, 1)
    t_from_x(0, 1)
    w_mid(1, 0)
    t_from_x(1, 1)
    gram_in_sib()

    my_cols = pl.ds(pl.multiple_of((zl * 2 + c) * kc, kc), kc)

    def gram(a, ref):
        lhs, rhs = ref[:, :, :, :, my_cols].reshape(n_tok, kc), ref[...].reshape(n_tok, BLOCK)
        out = lax.dot_general(lhs, rhs, (((0,), (0,)), ((), ())), preferred_element_type=F32)
        for z in range(4):
            for q in range(4):
                gp[a, q, z] = out[(z * 4 + q) * 16:(z * 4 + q + 1) * 16, :]
        for q in range(2):
            gbs[a, q] = gp[a, yy_of(1 - half, q)].astype(BF)

    w_mid(1, 1)
    for r, dev in ((3, xr), (1, xl), (2, xo)):
        recv(("gxo", r), xo_buf.at[c, zl, (x + 4 - r) % 4], dev)
    send("gzo", xo_buf.at[c, zl], xo_buf.at[c, zl], zlp)
    t_from_opp(0, 0)
    t_from_opp(1, 0)
    t_from_opp(0, 1)
    t_from_opp(1, 1)
    w_opp(1, 0)
    w_opp(1, 1)
    recv("gsi", xi.at[1 - c], sib)
    gram(0, xi)
    for p in range(2):
        cols = pl.ds(p * n_tok // 2, n_tok // 2)
        recv(("h", p), ht.at[1, :, cols], yb)
    send(("gb", 0), gbs.at[0], gbr.at[0], yb)

    for slot in range(2):
        for e in range(2):
            for r in range(4):
                recv(("ts", slot, e, r), tpiece(slot, e, (x + r) % 4, 1 - c), sib)

    scale = 1.0 / math.sqrt(total)

    def down(r, q):
        cols = pl.ds(pl.multiple_of((zz(r) * 2 + q) * kc, kc), kc)
        acc = jnp.dot(ht[0, :hd, :], tok[0, :, :, :, :, cols].reshape(n_tok, kc), preferred_element_type=F32)
        acc += jnp.dot(ht[1, :hd, :], tok[1, :, :, :, :, cols].reshape(n_tok, kc), preferred_element_type=F32)
        return acc * scale

    def dpiece(ref, i, p):
        return ref.at[i, pl.ds(p * hf, hf), :]

    def down_to_a(r, p):
        send(("da", r, p), dpiece(asnd, r, p), dpiece(arcv, r, p), ya)

    def first_rows():
        acc = jnp.dot(ht[0, hd:, :], tok[0].reshape(n_tok, kc * 8), preferred_element_type=F32)
        acc += jnp.dot(ht[1, hd:, :], tok[1].reshape(n_tok, kc * 8), preferred_element_type=F32)
        for j in range(8):
            fp[j] = acc[:, j * kc:(j + 1) * kc] * scale
        for q in range(2):
            fs1[q] = fp[zz(2) * 2 + q].astype(BF)
            send(("f1", q), fs1.at[q], f1.at[q], zr if q == 0 else zb)

    def first_rows_2():
        for q in range(2):
            recv(("f1", q), f1.at[q], zb if q == 0 else zr)
            r = 1 if q == 0 else 3
            fs2[q, q] = (fp[zz(r) * 2 + q] + f1[q].astype(F32)).astype(BF)
            fs2[q, 1 - q] = fp[zz(r) * 2 + 1 - q].astype(BF)
            send(("f2", q), fs2.at[q], f2.at[q], zr if q == 0 else zb)

    def first_sum(q):
        return fp[zh * 2 + q] + f2[0, q].astype(F32) + f2[1, q].astype(F32)

    def first_rows_to_a():
        recv(("f2", 0), f2.at[0], zb)
        recv(("f2", 1), f2.at[1], zr)
        fas[...] = first_sum(1 - s).astype(BF)
        send("fa", fas, far, ya)

    n_tile = n_tok // 2

    def hidden_grad(slot, hh, i):
        lhs = tok[slot, 2 * i:2 * i + 2].reshape(n_tile, kc * 8)
        rhs = wf0[...].reshape(kc * 8, SPLIT) if hh == 0 else wf1[...].reshape(kc * 8, ffl - SPLIT)
        return jnp.dot(lhs, rhs, preferred_element_type=F32)

    def hidden_to_b(hh, i):
        at = pl.ds(i * n_tile, n_tile)
        snd, rcv = (snd0, snd1)[hh], (rcv0, rcv1)[hh]
        send(("gh", hh, i), snd.at[at, :], rcv.at[at, :], yb)

    asnd[2] = down(2, 1 - s).astype(BF)
    down_to_a(2, 0)
    down_to_a(2, 1)
    first_rows()
    w_from_a(0)
    for i in range(2):
        snd0[i * n_tile:(i + 1) * n_tile, :] = hidden_grad(1, 0, i).astype(BF)
        hidden_to_b(0, i)
    asnd[1] = down(1, 1 - s).astype(BF)
    asnd[3] = down(3, 1 - s).astype(BF)
    part[2] = down(2, s)
    first_rows_2()
    w_from_a(1)
    for i in range(2):
        snd1[i * n_tile:(i + 1) * n_tile, :] = hidden_grad(1, 1, i).astype(BF)

    def reduced(r, p):
        recv(("da", r, p), dpiece(arcv, r, p), ya)
        at = pl.ds(p * hf, hf)
        return part[r, at, :] + arcv[r, at, :].astype(F32)

    def gram_to_a(a):
        recv(("gb", a), gbr.at[a], yb)
        gas[a] = (gp[a, yy_of(half, 1 - s)] + gbr[a, 1 - s].astype(F32)).astype(BF)
        send(("ga", a), gas.at[a], gar.at[a], ya)
        gf[a] = gp[a, yy_of(half, s)] + gbr[a, s].astype(F32)

    def gram_z1(a):
        recv(("ga", a), gar.at[a], ya)
        gf[a] = gf[a] + gar[a].astype(F32)
        gzs[a, 0] = gf[a, zz(2)].astype(BF)
        send(("gz1", a), gzs.at[a, 0], gz1.at[a], zr if a == 0 else zb)

    def gram_z2(a):
        recv(("gz1", a), gz1.at[a], zb if a == 0 else zr)
        passed = gz1[a].astype(F32)
        gzs[a, 1] = (gf[a, zz(1)] + passed if a == 0 else gf[a, zz(1)]).astype(BF)
        send(("gz2r", a), gzs.at[a, 1], gz2.at[a, 0], zr)
        gzs[a, 2] = (gf[a, zz(3)] + passed if a == 1 else gf[a, zz(3)]).astype(BF)
        send(("gz2l", a), gzs.at[a, 2], gz2.at[a, 1], zb)

    def gram_out(a, out, hbm):
        recv(("gz2r", a), gz2.at[a, 0], zb)
        recv(("gz2l", a), gz2.at[a, 1], zr)
        out[...] = (gf[a, zh] + gz2[a, 0].astype(F32) + gz2[a, 1].astype(F32)) / total
        store(out, hbm)

    gram_to_a(0)
    recv("gzo", xo_buf.at[c, 1 - zl], zlp)
    send("gso", xo_buf.at[c], xo_buf.at[c], sib)
    for q in range(2):
        mine = pl.ds(pl.multiple_of(yy_of(half, q) * kc, kc), kc)
        from_tok = pl.ds(pl.multiple_of((x * 2 + q) * kc, kc), kc)
        for cc in range(2):
            for zc in range(2):
                for xc in range(4):
                    gm[cc, zc, xc, :, mine] = tok[0, xc, zc, cc, :, from_tok]
    recv("gso", xo_buf.at[1 - c], sib)
    for q in range(2):
        other = pl.ds(pl.multiple_of(yy_of(1 - half, q) * kc, kc), kc)
        gm[:, :, :, :, other] = xo_buf[:, :, :, :, q * kc:(q + 1) * kc]
    gram(1, gm)
    send(("gb", 1), gbs.at[1], gbr.at[1], yb)
    hidden_to_b(1, 0)
    hidden_to_b(1, 1)

    zs[0] = reduced(2, 0).astype(BF)
    send(("z1", 0), zs.at[0], z1.at[0], zr)
    down_to_a(1, 1)
    down_to_a(3, 0)
    zs[1] = reduced(2, 1).astype(BF)
    send(("z1", 1), zs.at[1], z1.at[1], zb)
    down_to_a(1, 0)
    down_to_a(3, 1)
    first_rows_to_a()
    gram_z1(0)
    part[1] = down(1, s)
    part[3] = down(3, s)
    asnd[0] = down(0, 1 - s).astype(BF)
    gram_z2(0)
    gram_to_a(1)
    zs[2] = reduced(1, 1).astype(BF)
    send(("z2r", 1), zs.at[2], dpiece(z2, 0, 1), zr)
    zs[3] = reduced(3, 0).astype(BF)
    send(("z2l", 0), zs.at[3], dpiece(z2, 1, 0), zb)
    down_to_a(0, 0)
    down_to_a(0, 1)
    gram_z1(1)

    recv(("z1", 0), z1.at[0], zb)
    zs[4] = (reduced(1, 0) + z1[0].astype(F32)).astype(BF)
    send(("z2r", 0), zs.at[4], dpiece(z2, 0, 0), zr)
    recv(("z1", 1), z1.at[1], zr)
    zs[5] = (reduced(3, 1) + z1[1].astype(F32)).astype(BF)
    send(("z2l", 1), zs.at[5], dpiece(z2, 1, 1), zb)

    part[0] = down(0, s)
    for hh in range(2):
        for i in range(2):
            ghf[i * n_tile:(i + 1) * n_tile, hcols[hh]] = hidden_grad(0, hh, i)

    step = 32

    def finish(hh):
        rcv, cols = (rcv0, rcv1)[hh], hcols[hh]
        for i in range(2):
            at = pl.ds(i * n_tile, n_tile)
            recv(("gh", hh, i), rcv.at[at, :], yb)

            @pl.loop(0, n_tile // step)
            def _(k):
                rows_at = pl.ds(pl.multiple_of(i * n_tile + k * step, step), step)
                gh = ghf[rows_at, cols] + rcv[rows_at, :].astype(F32)
                gate = gate_ref[rows_at, cols].astype(F32)
                up = up_ref[rows_at, cols].astype(F32)
                sigma = jax.nn.sigmoid(gate)
                gu_ref[rows_at, cols] = (gh * (gate * sigma)).astype(BF)
                gg_ref[rows_at, cols] = (gh * up * sigma * (1.0 + gate * (1.0 - sigma))).astype(BF)

            store(gu_ref.at[at, cols], gu_hbm.at[at, cols])
            store(gg_ref.at[at, cols], gg_hbm.at[at, cols])

    finish(0)

    gram_z2(1)
    gram_out(0, gi_ref, gi_hbm)
    finish(1)
    gram_out(1, go_ref, go_hbm)

    last = pl.ds(hd, FIRST)
    recv("fa", far, ya)
    gd_ref[last, :] = (first_sum(s) + far[...].astype(F32)).astype(BF)
    store(gd_ref.at[last, :], gd_hbm.at[last, :])

    for p in range(2):
        at = pl.ds(p * hf, hf)
        recv(("z2r", p), dpiece(z2, 0, p), zb)
        recv(("z2l", p), dpiece(z2, 1, p), zr)
        own = reduced(0, p) + z2[0, at, :].astype(F32) + z2[1, at, :].astype(F32)
        gd_ref[at, :] = own.astype(BF)
        store(gd_ref.at[at, :], gd_hbm.at[at, :])

    for cp in started:
        cp.wait_send()
    for cp in stores:
        cp.wait()
    assert len(names) <= N_SEM and len(stores) <= 16, (len(names), len(stores))


PARTS = 4


def hand_over(*refs):
    ins, outs = [], []
    for i in range(5):
        src, dst, mid = refs[i], refs[5 + i], refs[10 + i]
        parts = PARTS if i < 3 else 1
        n = src.shape[0] // parts
        for p in range(parts):
            at = pl.ds(p * n, n)
            ins.append(pltpu.make_async_copy(src.at[at, :], mid.at[at, :], refs[15].at[i, p]))
            outs.append(pltpu.make_async_copy(mid.at[at, :], dst.at[at, :], refs[16].at[i, p]))
    for cp in ins:
        cp.start()
    for cp, out in zip(ins, outs):
        cp.wait()
        out.start()
    for cp in outs:
        cp.wait()


def shards(x_rows, grad_out, gate_pre, up_pre, down_weight):
    rows, width = x_rows.shape
    n_tok, ffl = gate_pre.shape
    kc = down_weight.shape[1]
    hd = ffl - FIRST
    hf = hd // 2
    total = float(rows * lax.axis_size("tensor") * lax.axis_size("dp"))
    gr = kc // 16
    hbm = pl.BlockSpec(memory_space=pl.ANY)

    def kern(*refs):
        kernel(total, *refs)

    outs = [
        ((n_tok, ffl), BF),
        ((n_tok, ffl), BF),
        ((ffl, kc), BF),
        ((gr, BLOCK), F32),
        ((gr, BLOCK), F32),
    ]
    results = pl.pallas_call(
        kern,
        out_shape=tuple(jax.ShapeDtypeStruct(*o) for o in outs),
        in_specs=[hbm] * 5,
        out_specs=(hbm,) * 5,
        scratch_shapes=[
            pltpu.VMEM((rows, width), BF),
            pltpu.VMEM((rows, width), BF),
            pltpu.VMEM((n_tok, ffl), BF),
            pltpu.VMEM((n_tok, ffl), BF),
            pltpu.VMEM((ffl, kc), BF),
            *(pltpu.VMEM(*o) for o in outs),
            pltpu.VMEM((rows, kc * 8), BF),
            pltpu.VMEM((2, 4, 2, 2, rows, kc * 8), BF),
            pltpu.VMEM((8, kc, SPLIT), BF),
            pltpu.VMEM((8, kc, ffl - SPLIT), BF),
            pltpu.VMEM((2, ffl, n_tok), BF),
            pltpu.VMEM((2, 2, 4, rows, BLOCK), BF),
            pltpu.VMEM((2, 2, 4, rows, 2 * kc), BF),
            pltpu.VMEM((2, 2, 4, rows, BLOCK), BF),
            pltpu.VMEM((4, hd, kc), BF),
            pltpu.VMEM((4, hd, kc), BF),
            pltpu.VMEM((4, hd, kc), F32),
            pltpu.VMEM((6, hf, kc), BF),
            pltpu.VMEM((2, hf, kc), BF),
            pltpu.VMEM((2, hd, kc), BF),
            pltpu.VMEM((8, FIRST, kc), F32),
            pltpu.VMEM((2, FIRST, kc), BF),
            pltpu.VMEM((2, 2, FIRST, kc), BF),
            pltpu.VMEM((2, FIRST, kc), BF),
            pltpu.VMEM((2, 2, FIRST, kc), BF),
            pltpu.VMEM((FIRST, kc), BF),
            pltpu.VMEM((FIRST, kc), BF),
            pltpu.VMEM((n_tok, SPLIT), BF),
            pltpu.VMEM((n_tok, ffl - SPLIT), BF),
            pltpu.VMEM((n_tok, SPLIT), BF),
            pltpu.VMEM((n_tok, ffl - SPLIT), BF),
            pltpu.VMEM((n_tok, ffl), F32),
            pltpu.VMEM((2, 4, 4, gr, BLOCK), F32),
            pltpu.VMEM((2, 2, 4, gr, BLOCK), BF),
            pltpu.VMEM((2, 2, 4, gr, BLOCK), BF),
            pltpu.VMEM((2, 4, gr, BLOCK), BF),
            pltpu.VMEM((2, 4, gr, BLOCK), BF),
            pltpu.VMEM((2, 4, gr, BLOCK), F32),
            pltpu.VMEM((2, 3, gr, BLOCK), BF),
            pltpu.VMEM((2, gr, BLOCK), BF),
            pltpu.VMEM((2, 2, gr, BLOCK), BF),
            pltpu.SemaphoreType.DMA((N_SEM,)),
            pltpu.SemaphoreType.DMA((N_SEM,)),
            pltpu.SemaphoreType.DMA((5,)),
            pltpu.SemaphoreType.DMA((16,)),
        ],
        compiler_params=pltpu.CompilerParams(
            collective_id=0, has_side_effects=True, vmem_limit_bytes=60 * 1024 * 1024
        ),
        cost_estimate=pl.CostEstimate(
            flops=4 * n_tok * width * ffl, bytes_accessed=8 * n_tok * ffl, transcendentals=0
        ),
    )(x_rows, grad_out, gate_pre, up_pre, down_weight)
    return pl.pallas_call(
        hand_over,
        out_shape=tuple(jax.ShapeDtypeStruct(*o) for o in outs),
        in_specs=[hbm] * 5,
        out_specs=(hbm,) * 5,
        scratch_shapes=[
            *(pltpu.VMEM(*o) for o in outs),
            pltpu.SemaphoreType.DMA((5, PARTS)),
            pltpu.SemaphoreType.DMA((5, PARTS)),
        ],
        compiler_params=pltpu.CompilerParams(vmem_limit_bytes=60 * 1024 * 1024),
    )(*results)


def solution(mesh):
    return jax.shard_map(
        shards,
        mesh=mesh,
        in_specs=(
            P(("dp", "tensor"), None),
            P(("dp", "tensor"), None),
            P("dp", "tensor"),
            P("dp", "tensor"),
            P("tensor", "dp"),
        ),
        out_specs=(
            P("dp", "tensor"),
            P("dp", "tensor"),
            P("tensor", "dp"),
            P(("tensor", "dp"), None),
            P(("tensor", "dp"), None),
        ),
        check_vma=False,
    )
```

```python
import math

import jax
import jax.numpy as jnp
from jax import lax
from jax.experimental import pallas as pl
from jax.experimental.pallas import tpu as pltpu
from jax.sharding import PartitionSpec as P

MESH = pl.DeviceIdType.MESH
BF = jnp.bfloat16
F32 = jnp.float32
BLOCK = 1024
N_SEM = 128
SPLIT = 512
FIRST = 192


def kernel(
    total,
    x_hbm, g_hbm, gate_hbm, up_hbm, w_hbm,
    gg_hbm, gu_hbm, gd_hbm, gi_hbm, go_hbm,
    x_ref, g_ref, gate_ref, up_ref, w_ref,
    gg_ref, gu_ref, gd_ref, gi_ref, go_ref,
    ghalf, tok, wf0, wf1, ht, xi, xo_buf, gm, asnd, arcv, part, zs, z1, z2,
    fp, fs1, fs2, f1, f2, fas, far,
    snd0, snd1, rcv0, rcv1, ghf, gp, gbs, gbr, gas, gar, gf, gzs, gz1, gz2,
    ssem, rsem, isem, osem,
):
    rows = g_ref.shape[0]
    ffl, kc = w_ref.shape
    n_tok = gate_ref.shape[0]
    hk = kc // 2
    hd = ffl - FIRST
    hf = hd // 2
    hcols = (pl.ds(0, SPLIT), pl.ds(SPLIT, ffl - SPLIT))
    d = lax.axis_index("dp")
    t = lax.axis_index("tensor")
    zh, y = d // 4, d % 4
    x, zl, c = t // 4, (t // 2) % 2, t % 2
    half = ((y + 1) // 2) % 2
    s = y // 2

    sib = (d, t + 1 - 2 * c)
    zlp = (d, t + 2 - 4 * zl)
    xr = (d, ((x + 1) % 4) * 4 + t % 4)
    xl = (d, ((x + 3) % 4) * 4 + t % 4)
    xo = (d, ((x + 2) % 4) * 4 + t % 4)
    ya = (zh * 4 + 3 - y, t)
    yb = (zh * 4 + y + 1 - 2 * (y % 2), t)
    zr = (((zh + 1) % 4) * 4 + y, t)
    zb = (((zh + 3) % 4) * 4 + y, t)
    zo = (((zh + 3 + 2 * zl) % 4) * 4 + y, t + 2 - 4 * zl)
    neighbours = (sib, zlp, zo, xr, xl, xo, ya, yb, zr, zb)

    barrier = pltpu.get_barrier_semaphore()
    for n in neighbours:
        pl.semaphore_signal(barrier, inc=1, device_id=n, device_id_type=MESH)
    loads = [
        pltpu.make_async_copy(a, b, isem.at[i])
        for i, (a, b) in enumerate(
            ((w_hbm, w_ref), (g_hbm, g_ref), (gate_hbm, gate_ref), (up_hbm, up_ref), (x_hbm, x_ref))
        )
    ]
    for cp in loads:
        cp.start()

    names = {}
    started = []
    stores = []

    def sem(key):
        return names.setdefault(key, len(names))

    def send(key, src_ref, dst_ref, dev):
        k = sem(key)
        cp = pltpu.make_async_remote_copy(
            src_ref=src_ref, dst_ref=dst_ref, send_sem=ssem.at[k], recv_sem=rsem.at[k],
            device_id=dev, device_id_type=MESH,
        )
        cp.start()
        started.append(cp)

    def recv(key, dst_ref, dev):
        k = sem(key)
        pltpu.make_async_remote_copy(
            src_ref=dst_ref, dst_ref=dst_ref, send_sem=ssem.at[k], recv_sem=rsem.at[k],
            device_id=dev, device_id_type=MESH,
        ).wait_recv()

    def store(src_ref, dst_ref):
        cp = pltpu.make_async_copy(src_ref, dst_ref, osem.at[len(stores)])
        cp.start()
        stores.append(cp)

    def zz(r):
        return (zh + r) % 4

    def yy_of(h, q):
        return h + q * (3 - 2 * h)

    def wpiece(r, q, hh, kh=None):
        ref = (wf0, wf1)[hh]
        if kh is None:
            return ref.at[zz(r) * 2 + q]
        return ref.at[zz(r) * 2 + q, pl.ds(kh * hk, hk), :]

    def w_to_a(r, hh, kh=None):
        send(("wa", r, hh, kh), wpiece(r, s, hh, kh), wpiece(r, s, hh, kh), ya)

    def w_own(hh, i):
        send(("wl", hh, i), wpiece(0, s, hh, i), wpiece(0, s, hh, i), zr)
        send(("wr", hh, i), wpiece(0, s, hh, 1 - i), wpiece(0, s, hh, 1 - i), zb)

    def w_mid(hh, i):
        recv(("wl", hh, i), wpiece(3, s, hh, i), zb)
        if i == 0:
            send(("wo", hh, 0), wpiece(3, s, hh, 0), wpiece(3, s, hh, 0), zr)
        recv(("wr", hh, i), wpiece(1, s, hh, 1 - i), zr)
        if i == 0:
            send(("wo", hh, 1), wpiece(1, s, hh, 1), wpiece(1, s, hh, 1), zb)
        w_to_a(3, hh, i)
        w_to_a(1, hh, 1 - i)

    def w_opp(hh, kh):
        recv(("wo", hh, kh), wpiece(2, s, hh, kh), zb if kh == 0 else zr)
        w_to_a(2, hh, kh)

    def w_from_a(hh):
        recv(("wa", 0, hh, None), wpiece(0, 1 - s, hh), ya)
        for r in (3, 1, 2):
            for kh in range(2):
                recv(("wa", r, hh, kh), wpiece(r, 1 - s, hh, kh), ya)

    loads[0].wait()
    wf0[zh * 2 + s] = w_ref[:SPLIT, :].astype(F32).T.astype(BF)
    wf1[zh * 2 + s] = w_ref[SPLIT:, :].astype(F32).T.astype(BF)

    loads[1].wait()
    for z in range(4):
        for q in range(2):
            to = pl.ds((z * 2 + q) * kc, kc)
            other = pl.multiple_of((z * 4 + yy_of(1 - half, q)) * kc, kc)
            mine = pl.multiple_of((z * 4 + yy_of(half, q)) * kc, kc)
            ghalf[:, to] = g_ref[:, pl.ds(other, kc)]
            tok[0, x, zl, c, :, to] = g_ref[:, pl.ds(mine, kc)]

    pl.semaphore_wait(barrier, len(neighbours))

    w_to_a(0, 0)
    w_own(0, 0)
    w_own(0, 1)

    def tpiece(slot, e, xx, cc=c):
        return tok.at[slot, xx, zl if e == 0 else 1 - zl, cc]

    x_left, x_right, x_opp = (x + 3) % 4, (x + 1) % 4, (x + 2) % 4

    def t_to_x(slot, e):
        ref = tpiece(slot, e, x)
        send(("txl", slot, e), ref, ref, xr)
        send(("txr", slot, e), ref, ref, xl)
        send(("ts", slot, e, 0), ref, ref, sib)

    wide = kc * 4

    def thalf(ref, p):
        return ref.at[:, pl.ds(p * wide, wide)]

    def t_from_x(slot, e):
        left, right = tpiece(slot, e, x_left), tpiece(slot, e, x_right)
        recv(("txl", slot, e), left, xl)
        send(("txo", slot, e, 0), thalf(left, 0), thalf(left, 0), xr)
        send(("ts", slot, e, 3), left, left, sib)
        recv(("txr", slot, e), right, xr)
        send(("txo", slot, e, 1), thalf(right, 1), thalf(right, 1), xl)
        send(("ts", slot, e, 1), right, right, sib)

    def t_from_opp(slot, e):
        opp = tpiece(slot, e, x_opp)
        recv(("txo", slot, e, 0), thalf(opp, 0), xl)
        recv(("txo", slot, e, 1), thalf(opp, 1), xr)
        send(("ts", slot, e, 2), opp, opp, sib)

    def t_to_z(slot):
        send(("tz", slot), tpiece(slot, 0, x), tpiece(slot, 0, x), zlp)

    send("tb", ghalf, tok.at[1, x, zl, c], yb)
    t_to_x(0, 0)
    w_to_a(0, 1)

    loads[2].wait()
    loads[3].wait()
    ht_tile = 128

    def hidden_tile(i):
        at = pl.ds(pl.multiple_of(i * ht_tile, ht_tile), ht_tile)
        gate = gate_ref[at, :].astype(F32)
        up = up_ref[at, :].astype(F32)
        hid = (gate * jax.nn.sigmoid(gate) * up).astype(BF)
        ht[0, :, at] = hid.astype(F32).T.astype(BF)

    n_ht = n_tok // ht_tile
    for p in range(2):
        pl.loop(p * n_ht // 2, (p + 1) * n_ht // 2)(hidden_tile)
        cols = pl.ds(p * n_tok // 2, n_tok // 2)
        send(("h", p), ht.at[0, :, cols], ht.at[1, :, cols], yb)

    loads[4].wait()

    def x_cols(xx):
        return pl.ds(pl.multiple_of(xx * BLOCK, BLOCK), BLOCK)

    def o_cols(xx):
        return pl.ds(pl.multiple_of(xx * 2 * kc, 2 * kc), 2 * kc)

    xi[c, zl, x] = x_ref[:, x_cols(x)]
    xo_buf[c, zl, x] = ghalf[:, o_cols(x)]
    for r, dev in ((1, xr), (3, xl), (2, xo)):
        send(("gxi", r), x_ref.at[:, x_cols((x + r) % 4)], xi.at[c, zl, x], dev)
        send(("gxo", r), ghalf.at[:, o_cols((x + r) % 4)], xo_buf.at[c, zl, x], dev)

    def gram_cols():
        for r, dev in ((3, xr), (1, xl), (2, xo)):
            recv(("gxi", r), xi.at[c, zl, (x + 4 - r) % 4], dev)
        send("gzi", xi.at[c, zl], xi.at[c, zl], zo)

    def gram_in_sib():
        recv("gzi", xi.at[c, 1 - zl], zo)
        send("gsi", xi.at[c], xi.at[c], sib)

    def tz_in(slot):
        recv(("tz", slot), tpiece(slot, 1, x), zlp)
        t_to_x(slot, 1)

    recv("tb", tpiece(1, 0, x), yb)
    t_to_x(1, 0)
    w_mid(0, 0)
    t_from_x(0, 0)
    t_to_z(0)
    w_mid(0, 1)
    t_to_z(1)
    gram_cols()
    t_from_x(1, 0)
    w_opp(0, 0)
    w_opp(0, 1)
    w_own(1, 0)
    tz_in(0)
    tz_in(1)
    w_own(1, 1)
    t_from_x(0, 1)
    w_mid(1, 0)
    t_from_x(1, 1)
    gram_in_sib()

    my_cols = pl.ds(pl.multiple_of((zl * 2 + c) * kc, kc), kc)

    def gram(a, ref):
        lhs, rhs = ref[:, :, :, :, my_cols].reshape(n_tok, kc), ref[...].reshape(n_tok, BLOCK)
        out = lax.dot_general(lhs, rhs, (((0,), (0,)), ((), ())), preferred_element_type=F32)
        for z in range(4):
            for q in range(4):
                gp[a, q, z] = out[(z * 4 + q) * 16:(z * 4 + q + 1) * 16, :]
        for q in range(2):
            gbs[a, q] = gp[a, yy_of(1 - half, q)].astype(BF)

    w_mid(1, 1)
    for r, dev in ((3, xr), (1, xl), (2, xo)):
        recv(("gxo", r), xo_buf.at[c, zl, (x + 4 - r) % 4], dev)
    send("gzo", xo_buf.at[c, zl], xo_buf.at[c, zl], zlp)
    t_from_opp(0, 0)
    t_from_opp(1, 0)
    t_from_opp(0, 1)
    t_from_opp(1, 1)
    w_opp(1, 0)
    w_opp(1, 1)
    recv("gsi", xi.at[1 - c], sib)
    gram(0, xi)
    for p in range(2):
        cols = pl.ds(p * n_tok // 2, n_tok // 2)
        recv(("h", p), ht.at[1, :, cols], yb)
    send(("gb", 0), gbs.at[0], gbr.at[0], yb)

    for slot in range(2):
        for e in range(2):
            for r in range(4):
                recv(("ts", slot, e, r), tpiece(slot, e, (x + r) % 4, 1 - c), sib)

    scale = 1.0 / math.sqrt(total)

    def down(r, q):
        cols = pl.ds(pl.multiple_of((zz(r) * 2 + q) * kc, kc), kc)
        acc = jnp.dot(ht[0, :hd, :], tok[0, :, :, :, :, cols].reshape(n_tok, kc), preferred_element_type=F32)
        acc += jnp.dot(ht[1, :hd, :], tok[1, :, :, :, :, cols].reshape(n_tok, kc), preferred_element_type=F32)
        return acc * scale

    def dpiece(ref, i, p):
        return ref.at[i, pl.ds(p * hf, hf), :]

    def down_to_a(r, p):
        send(("da", r, p), dpiece(asnd, r, p), dpiece(arcv, r, p), ya)

    def first_rows():
        acc = jnp.dot(ht[0, hd:, :], tok[0].reshape(n_tok, kc * 8), preferred_element_type=F32)
        acc += jnp.dot(ht[1, hd:, :], tok[1].reshape(n_tok, kc * 8), preferred_element_type=F32)
        for j in range(8):
            fp[j] = acc[:, j * kc:(j + 1) * kc] * scale
        for q in range(2):
            fs1[q] = fp[zz(2) * 2 + q].astype(BF)
            send(("f1", q), fs1.at[q], f1.at[q], zr if q == 0 else zb)

    def first_rows_2():
        for q in range(2):
            recv(("f1", q), f1.at[q], zb if q == 0 else zr)
            r = 1 if q == 0 else 3
            fs2[q, q] = (fp[zz(r) * 2 + q] + f1[q].astype(F32)).astype(BF)
            fs2[q, 1 - q] = fp[zz(r) * 2 + 1 - q].astype(BF)
            send(("f2", q), fs2.at[q], f2.at[q], zr if q == 0 else zb)

    def first_sum(q):
        return fp[zh * 2 + q] + f2[0, q].astype(F32) + f2[1, q].astype(F32)

    def first_rows_to_a():
        recv(("f2", 0), f2.at[0], zb)
        recv(("f2", 1), f2.at[1], zr)
        fas[...] = first_sum(1 - s).astype(BF)
        send("fa", fas, far, ya)

    n_tile = n_tok // 2

    def hidden_grad(slot, hh, i):
        lhs = tok[slot, 2 * i:2 * i + 2].reshape(n_tile, kc * 8)
        rhs = wf0[...].reshape(kc * 8, SPLIT) if hh == 0 else wf1[...].reshape(kc * 8, ffl - SPLIT)
        return jnp.dot(lhs, rhs, preferred_element_type=F32)

    def hidden_to_b(hh, i):
        at = pl.ds(i * n_tile, n_tile)
        snd, rcv = (snd0, snd1)[hh], (rcv0, rcv1)[hh]
        send(("gh", hh, i), snd.at[at, :], rcv.at[at, :], yb)

    asnd[2] = down(2, 1 - s).astype(BF)
    down_to_a(2, 0)
    down_to_a(2, 1)
    first_rows()
    w_from_a(0)
    for i in range(2):
        snd0[i * n_tile:(i + 1) * n_tile, :] = hidden_grad(1, 0, i).astype(BF)
        hidden_to_b(0, i)
    asnd[1] = down(1, 1 - s).astype(BF)
    asnd[3] = down(3, 1 - s).astype(BF)
    part[2] = down(2, s)
    first_rows_2()
    w_from_a(1)
    for i in range(2):
        snd1[i * n_tile:(i + 1) * n_tile, :] = hidden_grad(1, 1, i).astype(BF)

    def reduced(r, p):
        recv(("da", r, p), dpiece(arcv, r, p), ya)
        at = pl.ds(p * hf, hf)
        return part[r, at, :] + arcv[r, at, :].astype(F32)

    def gram_to_a(a):
        recv(("gb", a), gbr.at[a], yb)
        gas[a] = (gp[a, yy_of(half, 1 - s)] + gbr[a, 1 - s].astype(F32)).astype(BF)
        send(("ga", a), gas.at[a], gar.at[a], ya)
        gf[a] = gp[a, yy_of(half, s)] + gbr[a, s].astype(F32)

    def gram_z1(a):
        recv(("ga", a), gar.at[a], ya)
        gf[a] = gf[a] + gar[a].astype(F32)
        gzs[a, 0] = gf[a, zz(2)].astype(BF)
        send(("gz1", a), gzs.at[a, 0], gz1.at[a], zr if a == 0 else zb)

    def gram_z2(a):
        recv(("gz1", a), gz1.at[a], zb if a == 0 else zr)
        passed = gz1[a].astype(F32)
        gzs[a, 1] = (gf[a, zz(1)] + passed if a == 0 else gf[a, zz(1)]).astype(BF)
        send(("gz2r", a), gzs.at[a, 1], gz2.at[a, 0], zr)
        gzs[a, 2] = (gf[a, zz(3)] + passed if a == 1 else gf[a, zz(3)]).astype(BF)
        send(("gz2l", a), gzs.at[a, 2], gz2.at[a, 1], zb)

    def gram_out(a, out, hbm):
        recv(("gz2r", a), gz2.at[a, 0], zb)
        recv(("gz2l", a), gz2.at[a, 1], zr)
        out[...] = (gf[a, zh] + gz2[a, 0].astype(F32) + gz2[a, 1].astype(F32)) / total
        store(out, hbm)

    gram_to_a(0)
    recv("gzo", xo_buf.at[c, 1 - zl], zlp)
    send("gso", xo_buf.at[c], xo_buf.at[c], sib)
    for q in range(2):
        mine = pl.ds(pl.multiple_of(yy_of(half, q) * kc, kc), kc)
        from_tok = pl.ds(pl.multiple_of((x * 2 + q) * kc, kc), kc)
        for cc in range(2):
            for zc in range(2):
                for xc in range(4):
                    gm[cc, zc, xc, :, mine] = tok[0, xc, zc, cc, :, from_tok]
    recv("gso", xo_buf.at[1 - c], sib)
    for q in range(2):
        other = pl.ds(pl.multiple_of(yy_of(1 - half, q) * kc, kc), kc)
        gm[:, :, :, :, other] = xo_buf[:, :, :, :, q * kc:(q + 1) * kc]
    gram(1, gm)
    send(("gb", 1), gbs.at[1], gbr.at[1], yb)
    hidden_to_b(1, 0)
    hidden_to_b(1, 1)

    zs[0] = reduced(2, 0).astype(BF)
    send(("z1", 0), zs.at[0], z1.at[0], zr)
    down_to_a(1, 1)
    down_to_a(3, 0)
    zs[1] = reduced(2, 1).astype(BF)
    send(("z1", 1), zs.at[1], z1.at[1], zb)
    down_to_a(1, 0)
    down_to_a(3, 1)
    first_rows_to_a()
    gram_z1(0)
    part[1] = down(1, s)
    part[3] = down(3, s)
    asnd[0] = down(0, 1 - s).astype(BF)
    gram_z2(0)
    gram_to_a(1)
    zs[2] = reduced(1, 1).astype(BF)
    send(("z2r", 1), zs.at[2], dpiece(z2, 0, 1), zr)
    zs[3] = reduced(3, 0).astype(BF)
    send(("z2l", 0), zs.at[3], dpiece(z2, 1, 0), zb)
    down_to_a(0, 0)
    down_to_a(0, 1)
    gram_z1(1)

    recv(("z1", 0), z1.at[0], zb)
    zs[4] = (reduced(1, 0) + z1[0].astype(F32)).astype(BF)
    send(("z2r", 0), zs.at[4], dpiece(z2, 0, 0), zr)
    recv(("z1", 1), z1.at[1], zr)
    zs[5] = (reduced(3, 1) + z1[1].astype(F32)).astype(BF)
    send(("z2l", 1), zs.at[5], dpiece(z2, 1, 1), zb)

    part[0] = down(0, s)
    for hh in range(2):
        for i in range(2):
            ghf[i * n_tile:(i + 1) * n_tile, hcols[hh]] = hidden_grad(0, hh, i)

    step = 32

    def finish(hh):
        rcv, cols = (rcv0, rcv1)[hh], hcols[hh]
        for i in range(2):
            at = pl.ds(i * n_tile, n_tile)
            recv(("gh", hh, i), rcv.at[at, :], yb)

            @pl.loop(0, n_tile // step)
            def _(k):
                rows_at = pl.ds(pl.multiple_of(i * n_tile + k * step, step), step)
                gh = ghf[rows_at, cols] + rcv[rows_at, :].astype(F32)
                gate = gate_ref[rows_at, cols].astype(F32)
                up = up_ref[rows_at, cols].astype(F32)
                sigma = jax.nn.sigmoid(gate)
                gu_ref[rows_at, cols] = (gh * (gate * sigma)).astype(BF)
                gg_ref[rows_at, cols] = (gh * up * sigma * (1.0 + gate * (1.0 - sigma))).astype(BF)

            store(gu_ref.at[at, cols], gu_hbm.at[at, cols])
            store(gg_ref.at[at, cols], gg_hbm.at[at, cols])

    finish(0)

    gram_z2(1)
    gram_out(0, gi_ref, gi_hbm)
    finish(1)
    gram_out(1, go_ref, go_hbm)

    last = pl.ds(hd, FIRST)
    recv("fa", far, ya)
    gd_ref[last, :] = (first_sum(s) + far[...].astype(F32)).astype(BF)
    store(gd_ref.at[last, :], gd_hbm.at[last, :])

    for p in range(2):
        at = pl.ds(p * hf, hf)
        recv(("z2r", p), dpiece(z2, 0, p), zb)
        recv(("z2l", p), dpiece(z2, 1, p), zr)
        own = reduced(0, p) + z2[0, at, :].astype(F32) + z2[1, at, :].astype(F32)
        gd_ref[at, :] = own.astype(BF)
        store(gd_ref.at[at, :], gd_hbm.at[at, :])

    for cp in started:
        cp.wait_send()
    for cp in stores:
        cp.wait()
    assert len(names) <= N_SEM and len(stores) <= 16, (len(names), len(stores))


PARTS = 4


def hand_over(*refs):
    ins, outs = [], []
    for i in range(5):
        src, dst, mid = refs[i], refs[5 + i], refs[10 + i]
        parts = PARTS if i < 3 else 1
        n = src.shape[0] // parts
        for p in range(parts):
            at = pl.ds(p * n, n)
            ins.append(pltpu.make_async_copy(src.at[at, :], mid.at[at, :], refs[15].at[i, p]))
            outs.append(pltpu.make_async_copy(mid.at[at, :], dst.at[at, :], refs[16].at[i, p]))
    for cp in ins:
        cp.start()
    for cp, out in zip(ins, outs):
        cp.wait()
        out.start()
    for cp in outs:
        cp.wait()


def shards(x_rows, grad_out, gate_pre, up_pre, down_weight):
    rows, width = x_rows.shape
    n_tok, ffl = gate_pre.shape
    kc = down_weight.shape[1]
    hd = ffl - FIRST
    hf = hd // 2
    total = float(rows * lax.axis_size("tensor") * lax.axis_size("dp"))
    gr = kc // 16
    hbm = pl.BlockSpec(memory_space=pl.ANY)

    def kern(*refs):
        kernel(total, *refs)

    outs = [
        ((n_tok, ffl), BF),
        ((n_tok, ffl), BF),
        ((ffl, kc), BF),
        ((gr, BLOCK), F32),
        ((gr, BLOCK), F32),
    ]
    results = pl.pallas_call(
        kern,
        out_shape=tuple(jax.ShapeDtypeStruct(*o) for o in outs),
        in_specs=[hbm] * 5,
        out_specs=(hbm,) * 5,
        scratch_shapes=[
            pltpu.VMEM((rows, width), BF),
            pltpu.VMEM((rows, width), BF),
            pltpu.VMEM((n_tok, ffl), BF),
            pltpu.VMEM((n_tok, ffl), BF),
            pltpu.VMEM((ffl, kc), BF),
            *(pltpu.VMEM(*o) for o in outs),
            pltpu.VMEM((rows, kc * 8), BF),
            pltpu.VMEM((2, 4, 2, 2, rows, kc * 8), BF),
            pltpu.VMEM((8, kc, SPLIT), BF),
            pltpu.VMEM((8, kc, ffl - SPLIT), BF),
            pltpu.VMEM((2, ffl, n_tok), BF),
            pltpu.VMEM((2, 2, 4, rows, BLOCK), BF),
            pltpu.VMEM((2, 2, 4, rows, 2 * kc), BF),
            pltpu.VMEM((2, 2, 4, rows, BLOCK), BF),
            pltpu.VMEM((4, hd, kc), BF),
            pltpu.VMEM((4, hd, kc), BF),
            pltpu.VMEM((4, hd, kc), F32),
            pltpu.VMEM((6, hf, kc), BF),
            pltpu.VMEM((2, hf, kc), BF),
            pltpu.VMEM((2, hd, kc), BF),
            pltpu.VMEM((8, FIRST, kc), F32),
            pltpu.VMEM((2, FIRST, kc), BF),
            pltpu.VMEM((2, 2, FIRST, kc), BF),
            pltpu.VMEM((2, FIRST, kc), BF),
            pltpu.VMEM((2, 2, FIRST, kc), BF),
            pltpu.VMEM((FIRST, kc), BF),
            pltpu.VMEM((FIRST, kc), BF),
            pltpu.VMEM((n_tok, SPLIT), BF),
            pltpu.VMEM((n_tok, ffl - SPLIT), BF),
            pltpu.VMEM((n_tok, SPLIT), BF),
            pltpu.VMEM((n_tok, ffl - SPLIT), BF),
            pltpu.VMEM((n_tok, ffl), F32),
            pltpu.VMEM((2, 4, 4, gr, BLOCK), F32),
            pltpu.VMEM((2, 2, 4, gr, BLOCK), BF),
            pltpu.VMEM((2, 2, 4, gr, BLOCK), BF),
            pltpu.VMEM((2, 4, gr, BLOCK), BF),
            pltpu.VMEM((2, 4, gr, BLOCK), BF),
            pltpu.VMEM((2, 4, gr, BLOCK), F32),
            pltpu.VMEM((2, 3, gr, BLOCK), BF),
            pltpu.VMEM((2, gr, BLOCK), BF),
            pltpu.VMEM((2, 2, gr, BLOCK), BF),
            pltpu.SemaphoreType.DMA((N_SEM,)),
            pltpu.SemaphoreType.DMA((N_SEM,)),
            pltpu.SemaphoreType.DMA((5,)),
            pltpu.SemaphoreType.DMA((16,)),
        ],
        compiler_params=pltpu.CompilerParams(
            collective_id=0, has_side_effects=True, vmem_limit_bytes=60 * 1024 * 1024
        ),
        cost_estimate=pl.CostEstimate(
            flops=4 * n_tok * width * ffl, bytes_accessed=8 * n_tok * ffl, transcendentals=0
        ),
    )(x_rows, grad_out, gate_pre, up_pre, down_weight)
    return pl.pallas_call(
        hand_over,
        out_shape=tuple(jax.ShapeDtypeStruct(*o) for o in outs),
        in_specs=[hbm] * 5,
        out_specs=(hbm,) * 5,
        scratch_shapes=[
            *(pltpu.VMEM(*o) for o in outs),
            pltpu.SemaphoreType.DMA((5, PARTS)),
            pltpu.SemaphoreType.DMA((5, PARTS)),
        ],
        compiler_params=pltpu.CompilerParams(vmem_limit_bytes=60 * 1024 * 1024),
    )(*results)


def solution(mesh):
    return jax.shard_map(
        shards,
        mesh=mesh,
        in_specs=(
            P(("dp", "tensor"), None),
            P(("dp", "tensor"), None),
            P("dp", "tensor"),
            P("dp", "tensor"),
            P("tensor", "dp"),
        ),
        out_specs=(
            P("dp", "tensor"),
            P("dp", "tensor"),
            P("tensor", "dp"),
            P(("tensor", "dp"), None),
            P(("tensor", "dp"), None),
        ),
        check_vma=False,
    )
```
